32 devices in a mesh: dp: 8 (over z, core), expert: 4 (over y, x).
Axes of the slice: x: 2, y: 2, z: 4, core: 2. Of those that a mesh axis runs over, the one named last changes fastest.
Arguments:
- tokens: bfloat16 [384, 4096], P('dp', 'expert'), may hold values from -6 to 6
- picks: int32 [384, 8], P('dp'), may hold values from 0 to 127, all different within a row; in each aligned block of 48 rows (0 to 47, 48 to 95, ...) at most 6 rows name the same one
- gates: float32 [384, 8], P('dp'), may hold values from 0.05 to 0.5
- w_gate: bfloat16 [8, 4096, 1536], P('dp', 'expert'), may hold values from -0.09375 to 0.09375
- w_up: bfloat16 [8, 4096, 1536], P('dp', 'expert'), may hold values from -0.09375 to 0.09375
- w_down: bfloat16 [8, 1536, 4096], P('dp', None, 'expert'), may hold values from -0.15625 to 0.15625
- cotangent: bfloat16 [384, 4096], P('dp', 'expert'), may hold values from -6 to 6
Outputs:
- mixed: bfloat16 [384, 4096], P('dp', 'expert')
- grad_tokens: bfloat16 [384, 4096], P('dp', 'expert')
- grad_gates: float32 [384, 8], P('dp')
The draws below stay inside these ranges and needn't reach their ends.
Inputs may be any that keep to these rules, and one draw needn't show every extreme that they name: Among the 48 tokens of one index of dp, no expert is named by more than 6 picks, a bound that some block reaches; the 8 picks of a token differ.
All inputs are finite; a program needn't handle non-finite values.
Results may differ from the reference program's by a relative error of at most 0.0064.
Values may be sent and summed in bfloat16 or wider, within the bound.
A program may use at most 64 MiB of HBM per device.

```python
import math
import jax
import jax.numpy as jnp
import numpy as np
from jax import lax

D = 4096
H = 1536
ROUTED = 128
TOP = 8
TOK_ROW = 48
CAP = 6
EXPERTS = 8
TOKENS = 384
N_DP = 8


def levels(key, dims, shards, least, high):
    def one(dim, parts):
        draws = jax.random.uniform(jax.random.fold_in(jax.random.fold_in(key, 6), dim), (parts,), jnp.float32, least / len(shards), high / len(shards))
        return jnp.repeat(jnp.exp(draws), dims[dim] // parts).reshape((-1,) + (1,) * (len(dims) - dim - 1))

    level = one(*shards[0])
    for cut in shards[1:]:
        level = level * one(*cut)
    return level


def deal_out(rng, own, number, rows, count, top, bound, slope):
    ranking = jax.random.permutation(rng, count)
    heavy_load, ordinary = load_shares(count, rows * top, bound, slope, True), load_shares(count, rows * top, bound, slope, False)
    places = jnp.arange(count)

    def named(sizes, offset_by):
        used = int((sizes > 0).sum())
        fixed = max(1, used // 4)
        moved = fixed + (places - fixed + offset_by * (used - fixed)) % max(1, count - fixed)
        return jnp.zeros((count,), jnp.int32).at[ranking[jnp.where(places < fixed, places, moved)]].set(jnp.asarray(sizes, jnp.int32))

    sizes = jnp.where(number % 4 == 0, named(heavy_load, number // 4), named(ordinary, number - number // 4 - 1))
    mixed = jax.random.permutation(jax.random.fold_in(own, 3), count)
    source_of, taker = mixed[0:count // 2 * 2:2], mixed[1:count // 2 * 2:2]
    margin = jnp.minimum(sizes[source_of] - 1, bound - sizes[taker]) // 2
    margin = jnp.where((source_of == ranking[0]) | (taker == ranking[0]) | (sizes[taker] == 0), 0, jnp.maximum(margin, 0))
    moved = jax.random.randint(jax.random.fold_in(own, 4), (count // 2,), 0, 1 << 20) % (margin + 1)
    sizes = sizes.at[source_of].add(-moved).at[taker].add(moved)
    members = jnp.searchsorted(jnp.cumsum(sizes), jnp.arange(rows * top), side="right").astype(jnp.int32)
    grid = members.reshape(top, rows).T
    grid = grid[jax.random.permutation(jax.random.fold_in(own, 1), rows)]
    offset_by = jax.random.randint(jax.random.fold_in(own, 2), (rows, 1), 0, top)
    return jnp.take_along_axis(grid, (jnp.arange(top)[None, :] + offset_by) % top, axis=1)


def load_shares(count, total, reach, skew, full):
    loads = [(1 << 20) // math.isqrt(standing ** skew) + 1 for standing in range(1, count + 1)]
    largest = reach if full else min(reach, max(-(-total // count), total * loads[0] // sum(loads)))
    least = 1 if total - largest >= count - 1 else 0
    given, rest = [largest] + [least] * (count - 1), total - largest - least * (count - 1)
    while rest > 0:
        candidates = [i for i in range(1, count) if given[i] < largest] or [i for i in range(1, count) if given[i] < reach]
        whole, remaining = sum([loads[i] for i in candidates]), rest
        for i in candidates:
            addition = min(reach - given[i], max(1, remaining * loads[i] // whole), rest)
            given[i] = given[i] + addition
            rest = rest - addition
    return np.array(given)


def scatter_about(key, shape, scale, bound, cuts=(), held_as=jnp.bfloat16):
    entries = jax.random.normal(key, shape, jnp.float32) * scale
    if len(cuts) > 0:
        entries = levels(key, shape, cuts, -0.22, 0.18) * entries
    return jnp.clip(entries, min=-bound, max=bound).astype(held_as)


def setup_inputs(seed: int = 0) -> dict:
    key_of = jax.random.split(jax.random.key(seed), 8)
    tokens = scatter_about(key_of[0], (TOKENS, D), 1.0, 6.0, ((0, 8), (1, 4)))
    picks_keys = jax.random.split(jax.random.fold_in(key_of[1], 1), TOKENS // TOK_ROW)
    picks_turns = jax.random.permutation(jax.random.fold_in(key_of[1], 3), TOKENS // TOK_ROW)
    picks = jax.vmap(lambda own, number: deal_out(jax.random.fold_in(key_of[1], 2), own, number, TOK_ROW, ROUTED, TOP, CAP, 2))(picks_keys, picks_turns).reshape((TOKENS, TOP))
    gates = jnp.clip(jnp.exp(math.log(0.5) - 2.3025851 * jax.random.uniform(key_of[2], (TOKENS, TOP), jnp.float32) ** levels(key_of[2], (TOKENS, TOP), ((0, 8),), -0.2, 0.2)), 0.05, 0.5)
    w_gate = scatter_about(key_of[3], (EXPERTS, D, H), D ** -0.5, 0.09375, ((0, 8), (1, 4)))
    w_up = scatter_about(key_of[4], (EXPERTS, D, H), D ** -0.5, 0.09375, ((0, 8), (1, 4)))
    w_down = scatter_about(key_of[5], (EXPERTS, H, D), H ** -0.5, 0.15625, ((0, 8), (2, 4)))
    cotangent = scatter_about(key_of[6], (TOKENS, D), 1.0, 6.0, ((0, 8), (1, 4)))
    return dict(tokens=tokens, picks=picks, gates=gates, w_gate=w_gate, w_up=w_up, w_down=w_down, cotangent=cotangent)


def silu_parts(gate_pre):
    logistic = jax.nn.sigmoid(gate_pre)
    return gate_pre * logistic, logistic * (1.0 + gate_pre * (1.0 - logistic))


def expert_pass(inputs):
    tok_in, grad_in, gate_mat, up_mat, down_mat = inputs
    gate_pre = jnp.dot(tok_in, gate_mat, preferred_element_type=jnp.float32)
    up_pre = jnp.dot(tok_in, up_mat, preferred_element_type=jnp.float32)
    silu_val, silu_slope = silu_parts(gate_pre)
    hidden_act = (silu_val * up_pre).astype(jnp.bfloat16)
    expert_out = jnp.dot(hidden_act, down_mat, preferred_element_type=jnp.float32).astype(jnp.bfloat16)
    grad_hidden = jnp.dot(grad_in, down_mat.T, preferred_element_type=jnp.float32)
    grad_gate = (grad_hidden * up_pre * silu_slope).astype(jnp.bfloat16)
    grad_up = (grad_hidden * silu_val).astype(jnp.bfloat16)
    grad_pick = jnp.dot(grad_gate, gate_mat.T, preferred_element_type=jnp.float32)
    grad_pick = grad_pick + jnp.dot(grad_up, up_mat.T, preferred_element_type=jnp.float32)
    return expert_out, grad_pick.astype(jnp.bfloat16)


def reference(tokens, picks, gates, w_gate, w_up, w_down, cotangent):
    pair_count = TOK_ROW * TOP
    slot_total = N_DP * CAP
    row_picks = picks.reshape(N_DP, pair_count)
    onehot = (row_picks[:, :, None] == jnp.arange(ROUTED, dtype=jnp.int32)[None, None, :]).astype(jnp.int32)
    slot_rank = jnp.sum((jnp.cumsum(onehot, axis=1) - onehot) * onehot, axis=2)
    in_window = row_picks < EXPERTS
    row_ids = jnp.arange(N_DP, dtype=jnp.int32)[:, None]
    slot_index = (row_picks * N_DP + row_ids) * CAP + slot_rank
    limit = EXPERTS * slot_total
    slot_index = jnp.where(in_window, slot_index, limit).reshape(-1).astype(jnp.int32)
    token_id = (jnp.arange(TOKENS * TOP, dtype=jnp.int32) // TOP).astype(jnp.int32)
    pair_tok = tokens[token_id]
    pair_grad = (gates.reshape(-1, 1) * cotangent[token_id].astype(jnp.float32)).astype(jnp.bfloat16)
    tok_slots = jnp.zeros((limit, D), jnp.bfloat16).at[slot_index].set(pair_tok, mode="drop")
    grad_slots = jnp.zeros((limit, D), jnp.bfloat16).at[slot_index].set(pair_grad, mode="drop")
    outs, grads = lax.map(expert_pass, (tok_slots.reshape(EXPERTS, slot_total, D), grad_slots.reshape(EXPERTS, slot_total, D), w_gate, w_up, w_down))
    outs = outs.reshape(limit, D)
    grads = grads.reshape(limit, D)
    clipped = jnp.minimum(slot_index, limit - 1).astype(jnp.int32)
    live = in_window.reshape(-1, 1)
    pair_out = jnp.where(live, outs[clipped].astype(jnp.float32), 0.0).reshape(TOKENS, TOP, D)
    pair_dx = jnp.where(live, grads[clipped].astype(jnp.float32), 0.0).reshape(TOKENS, TOP, D)
    mixed = jnp.sum(gates[:, :, None] * pair_out, axis=1).astype(jnp.bfloat16)
    grad_tokens = jnp.sum(pair_dx, axis=1).astype(jnp.bfloat16)
    grad_gates = jnp.sum(cotangent.astype(jnp.float32)[:, None, :] * pair_out, axis=2)
    return mixed, grad_tokens, grad_gates
```

```python
import functools

import jax
import jax.numpy as jnp
from jax import lax
from jax.experimental import pallas as pl
from jax.experimental.pallas import tpu as pltpu
from jax.sharding import PartitionSpec as P

CAP = 6
ROWS = 16
BF16 = jnp.bfloat16
F32 = jnp.float32
NN = (((1,), (0,)), ((), ()))
NT = (((1,), (1,)), ((), ()))
TN = (((0,), (0,)), ((), ()))


def mm(a, b, dims=NN):
    return lax.dot_general(a, b, dims, preferred_element_type=F32)


def iota(shape, dim):
    return lax.broadcasted_iota(jnp.int32, shape, dim)


def onehot(mask):
    return jnp.where(mask, 1.0, 0.0).astype(BF16)


def layer(
    n, m, tokens, picks, gates, w_gate, w_up, w_down, cotangent,
    mixed, grad_tokens, grad_gates,
    gate_v, up_v, down_v, send, recv, part, part_in, hid, hid_in, dot_out, dot_in, ret, back,
    w_sem, send_sem, recv_sem, ex_send, ex_recv,
):
    me = lax.axis_index("dp")
    mine = lax.axis_index("expert")
    tok, feat = tokens.shape
    top = picks.shape[1]
    slots = n * CAP
    cols = n * ROWS
    hid_c = part.shape[2] // 3

    def ring(index, step, size):
        return lax.rem(index + (step % size), size)

    loads = [
        pltpu.make_async_copy(src.at[0], dst, w_sem.at[i])
        for i, (src, dst) in enumerate(((w_gate, gate_v), (w_up, up_v), (w_down, down_v)))
    ]
    for load in loads:
        load.start()

    barrier = pltpu.get_barrier_semaphore()
    for o in range(1, n):
        pl.semaphore_signal(barrier, inc=1, device_id={"dp": ring(me, o, n)})
    for o in range(1, m):
        pl.semaphore_signal(barrier, inc=1, device_id={"expert": ring(mine, o, m)})

    col = iota((tok, cols), 1)
    named = me + (col >> 4)
    named = jnp.where(named >= n, named - n, named)
    picked = jnp.zeros((tok, cols), F32)
    gate_of = jnp.zeros((tok, cols), F32)
    for k in range(top):
        hit = picks[:, k : k + 1] == named
        picked = jnp.where(hit, 1.0, picked)
        gate_of = jnp.where(hit, gates[:, k : k + 1], gate_of)
    earlier = onehot(iota((tok, tok), 1) < iota((tok, tok), 0))
    rank = mm(earlier, picked.astype(BF16))
    row = col & 15
    chosen = (picked > 0.5) & (rank == (col & 7).astype(F32))
    forward = row < 8
    sel_tok = onehot(chosen & forward)
    sel_cot = onehot(chosen & (row >= 8))
    weight = jnp.where(chosen & forward, gate_of, 0.0)
    row_gate = jnp.sum(jnp.where(chosen, gate_of, 0.0), axis=0, keepdims=True)
    eye = iota((cols, cols), 0) == iota((cols, cols), 1)
    col_gate = jnp.sum(jnp.where(eye, row_gate, 0.0), axis=1, keepdims=True)
    out_rows = mm(sel_tok, tokens[...], TN) + mm(sel_cot, cotangent[...], TN) * col_gate
    send[...] = out_rows.astype(BF16).reshape(n, ROWS, feat)

    pl.semaphore_wait(barrier, n - 1 + m - 1)
    order = sorted(range(1, n), key=lambda o: -min(o, n - o))
    going = {}
    for o in order:
        going[o] = pltpu.make_async_remote_copy(
            src_ref=send.at[o], dst_ref=recv.at[o],
            send_sem=send_sem.at[0, o], recv_sem=recv_sem.at[0, o],
            device_id={"dp": ring(me, o, n)},
        )
        going[o].start()
    recv[0] = send[0]

    weight_hi = weight.astype(BF16)
    weight_lo = (weight - weight_hi.astype(F32)).astype(BF16)
    mix = jnp.concatenate([weight_hi, weight_lo, sel_cot], axis=0)
    dot_row = (row == 6) | (row == 7) | (row == 14)
    dot_pick = []
    dot_rank = []
    for k in range(top):
        hit = picks[:, k : k + 1] == named
        dot_pick.append(onehot(hit & dot_row))
        dot_rank.append(
            jnp.sum(jnp.where(hit & (row == 0), rank, 0.0), axis=1, keepdims=True)
        )

    slot_j = iota((slots, cols), 0)
    slot_c = iota((slots, cols), 1)
    here = (slot_c >> 4) * CAP + (slot_c & 7) == slot_j
    here = here & ((slot_c & 7) < CAP)
    pack_tok = onehot(here & ((slot_c & 15) < 8))
    pack_cot = onehot(here & ((slot_c & 15) >= 8))

    for o in order:
        going[o].wait_recv()
    got = recv[...].reshape(cols, feat)
    x_tok = mm(pack_tok, got).astype(BF16)
    x_cot = mm(pack_cot, got).astype(BF16)

    for load in loads:
        load.wait()

    def products(owner):
        at = pl.ds(pl.multiple_of(owner * hid_c, 128), hid_c)
        return (
            mm(x_tok, gate_v[:, at]),
            mm(x_tok, up_v[:, at]),
            mm(x_cot, down_v[at, :], NT),
        )

    steps = [m // 2] + [o for o in range(1, m) if o != m // 2] if m > 1 else []
    summing = {}
    for o in steps:
        for i, value in enumerate(products(ring(mine, o, m))):
            part[o, :, i * hid_c : (i + 1) * hid_c] = value.astype(BF16)
        summing[o] = pltpu.make_async_remote_copy(
            src_ref=part.at[o], dst_ref=part_in.at[o],
            send_sem=ex_send.at[0, o], recv_sem=ex_recv.at[0, o],
            device_id={"expert": ring(mine, o, m)},
        )
        summing[o].start()
    gate_pre, up_pre, grad_hidden = products(mine)
    for o in steps:
        summing[o].wait_recv()
        gate_pre += part_in[o, :, :hid_c].astype(F32)
        up_pre += part_in[o, :, hid_c : 2 * hid_c].astype(F32)
        grad_hidden += part_in[o, :, 2 * hid_c :].astype(F32)

    logistic = jax.nn.sigmoid(gate_pre)
    silu = gate_pre * logistic
    act = (silu * up_pre).astype(BF16)
    hid[:, :hid_c] = act
    hid[:, hid_c : 2 * hid_c] = (
        grad_hidden * up_pre * (logistic * (1.0 + gate_pre * (1.0 - logistic)))
    ).astype(BF16)
    hid[:, 2 * hid_c :] = (grad_hidden * silu).astype(BF16)
    spread = {}
    for o in steps:
        spread[o] = pltpu.make_async_remote_copy(
            src_ref=hid, dst_ref=hid_in.at[o],
            send_sem=ex_send.at[1, o], recv_sem=ex_recv.at[1, o],
            device_id={"expert": ring(mine, o, m)},
        )
        spread[o].start()
    dots = jnp.sum(act.astype(F32) * grad_hidden, axis=1, keepdims=True)
    wide = dot_out.shape[1]
    diag = iota((slots, wide), 0) == iota((slots, wide), 1)
    dots = jnp.sum(jnp.where(diag, dots, 0.0), axis=0, keepdims=True)
    dot_out[...] = jnp.broadcast_to(dots, dot_out.shape)
    spread_dot = {}
    for o in steps:
        spread_dot[o] = pltpu.make_async_remote_copy(
            src_ref=dot_out, dst_ref=dot_in.at[o],
            send_sem=ex_send.at[2, o], recv_sem=ex_recv.at[2, o],
            device_id={"expert": ring(mine, o, m)},
        )
        spread_dot[o].start()

    def backward(block, owner):
        at = pl.ds(pl.multiple_of(owner * hid_c, 128), hid_c)
        out = mm(block[:, :hid_c], down_v[at, :])
        grad = mm(block[:, hid_c : 2 * hid_c], gate_v[:, at], NT)
        grad += mm(block[:, 2 * hid_c :], up_v[:, at], NT)
        return out, grad

    out, grad = backward(hid, mine)
    for o in reversed(steps):
        spread[o].wait_recv()
        more_out, more_grad = backward(hid_in.at[o], ring(mine, m - o, m))
        out += more_out
        grad += more_grad
    for o in steps:
        spread_dot[o].wait_recv()
        dots += dot_in[o, 0:1, :]

    back_c = iota((cols, slots), 0)
    back_j = iota((cols, slots), 1)
    home = (back_c >> 4) * CAP
    place = (home + (back_c & 7) == back_j) & ((back_c & 7) < CAP)
    blocks = mm(onehot(place & ((back_c & 15) < 8)), out.astype(BF16))
    blocks += mm(onehot(place & ((back_c & 15) >= 8)), grad.astype(BF16))
    ret[...] = blocks.astype(BF16).reshape(n, ROWS, feat)
    dots = jnp.sum(jnp.where(diag, dots, 0.0), axis=1, keepdims=True)
    lane_j = iota((slots, 128), 0)
    lane = iota((slots, 128), 1)
    spot = lane == lane_j - CAP * ((lane_j * 10923) >> 16)
    rest = jnp.where(spot, dots, 0.0)
    family = (back_j >= home) & (back_j < home + CAP)
    terms = jnp.zeros((cols, 128), F32)
    for r in (6, 7, 14):
        term = rest.astype(BF16)
        rest = rest - term.astype(F32)
        terms += mm(onehot(family & ((back_c & 15) == r)), term)
    ret[:, :, :128] = (blocks[:, :128] + terms).astype(BF16).reshape(n, ROWS, 128)

    home_bound = {}
    for o in order:
        home_bound[o] = pltpu.make_async_remote_copy(
            src_ref=ret.at[o], dst_ref=back.at[o],
            send_sem=send_sem.at[1, o], recv_sem=recv_sem.at[1, o],
            device_id={"dp": ring(me, n - o, n)},
        )
        home_bound[o].start()
    back[0] = ret[0]
    for o in order:
        home_bound[o].wait_recv()
    rows = back[...].reshape(cols, feat)
    total = mm(mix, rows)
    mixed[...] = (total[:tok] + total[tok : 2 * tok]).astype(BF16)
    grad_tokens[...] = total[2 * tok :].astype(BF16)
    found = mm(jnp.concatenate(dot_pick, axis=0), rows[:, :128])
    lane = iota((tok, 128), 1).astype(F32)
    for k in range(top):
        value = jnp.where(lane == dot_rank[k], found[k * tok : (k + 1) * tok], 0.0)
        grad_gates[:, k : k + 1] = (
            jnp.sum(value, axis=1, keepdims=True) / gates[:, k : k + 1]
        )

    for o in order:
        going[o].wait_send()
        home_bound[o].wait_send()
    for o in steps:
        summing[o].wait_send()
        spread[o].wait_send()
        spread_dot[o].wait_send()


def shards(tokens, picks, gates, w_gate, w_up, w_down, cotangent):
    n = lax.axis_size("dp")
    m = lax.axis_size("expert")
    tok, feat = tokens.shape
    hidden = w_gate.shape[2]
    slots = n * CAP
    share = hidden // m
    hid_c = -(-share // 128) * 128
    if hid_c != share:
        fill = hid_c - share
        w_gate, w_up = (
            jnp.pad(w.reshape(1, feat, m, share), ((0, 0), (0, 0), (0, 0), (0, fill))).reshape(
                1, feat, m * hid_c
            )
            for w in (w_gate, w_up)
        )
        w_down = jnp.pad(
            w_down.reshape(1, m, share, feat), ((0, 0), (0, 0), (0, fill), (0, 0))
        ).reshape(1, m * hid_c, feat)
    wide = -(-slots // 128) * 128
    vmem = pl.BlockSpec(memory_space=pltpu.VMEM)
    hbm = pl.BlockSpec(memory_space=pl.ANY)
    dma = pltpu.SemaphoreType.DMA
    return pl.pallas_call(
        functools.partial(layer, n, m),
        out_shape=(
            jax.ShapeDtypeStruct(tokens.shape, BF16),
            jax.ShapeDtypeStruct(tokens.shape, BF16),
            jax.ShapeDtypeStruct(gates.shape, F32),
        ),
        in_specs=[vmem, vmem, vmem, hbm, hbm, hbm, vmem],
        out_specs=(vmem, vmem, vmem),
        scratch_shapes=[
            pltpu.VMEM((feat, m * hid_c), BF16),
            pltpu.VMEM((feat, m * hid_c), BF16),
            pltpu.VMEM((m * hid_c, feat), BF16),
            pltpu.VMEM((n, ROWS, feat), BF16),
            pltpu.VMEM((n, ROWS, feat), BF16),
            pltpu.VMEM((m, slots, 3 * hid_c), BF16),
            pltpu.VMEM((m, slots, 3 * hid_c), BF16),
            pltpu.VMEM((slots, 3 * hid_c), BF16),
            pltpu.VMEM((m, slots, 3 * hid_c), BF16),
            pltpu.VMEM((8, wide), F32),
            pltpu.VMEM((m, 8, wide), F32),
            pltpu.VMEM((n, ROWS, feat), BF16),
            pltpu.VMEM((n, ROWS, feat), BF16),
            dma((3,)),
            dma((2, n)),
            dma((2, n)),
            dma((3, m)),
            dma((3, m)),
        ],
        compiler_params=pltpu.CompilerParams(
            collective_id=0, has_side_effects=True, vmem_limit_bytes=56 * 1024 * 1024
        ),
    )(tokens, picks, gates, w_gate, w_up, w_down, cotangent)


def solution(mesh):
    placed = (
        P("dp", "expert"),
        P("dp", None),
        P("dp", None),
        P("dp", "expert", None),
        P("dp", "expert", None),
        P("dp", None, "expert"),
        P("dp", "expert"),
    )
    return jax.shard_map(
        shards,
        mesh=mesh,
        in_specs=placed,
        out_specs=(P("dp", "expert"), P("dp", "expert"), P("dp", None)),
        check_vma=False,
    )
```

```python
import functools

import jax
import jax.numpy as jnp
from jax import lax
from jax.experimental import pallas as pl
from jax.experimental.pallas import tpu as pltpu
from jax.sharding import PartitionSpec as P

CAP = 6
ROWS = 16
LANES = 128
BF16 = jnp.bfloat16
F32 = jnp.float32
NN = (((1,), (0,)), ((), ()))
NT = (((1,), (1,)), ((), ()))
TN = (((0,), (0,)), ((), ()))


def mm(a, b, dims=NN):
    return lax.dot_general(a, b, dims, preferred_element_type=F32)


def iota(shape, dim):
    return lax.broadcasted_iota(jnp.int32, shape, dim)


def onehot(mask):
    return jnp.where(mask, 1.0, 0.0).astype(BF16)


def spread_tiles(tiles):
    wide = -(-tiles * CAP // ROWS)
    return [
        sorted({i // CAP for i in range(w * ROWS, min((w + 1) * ROWS, tiles * CAP))})
        for w in range(wide)
    ]


def sixth(value):
    return (value * 10923) >> 16


def fold_maps(slots, blocks, tiles):
    maps = []
    for w, found in enumerate(spread_tiles(tiles)):
        shape = (blocks * ROWS, len(found) * slots)
        row, lane = iota(shape, 0), iota(shape, 1)
        number = (row & (ROWS - 1)) + w * ROWS
        tile = sixth(number)
        target = (tile - found[0]) * slots + (row >> 4) * CAP + number - tile * CAP
        maps.append(onehot((lane == target) & (number < tiles * CAP)))
    return maps


def fold(maps, value, blocks):
    tiles = value.shape[1] // LANES
    parts = []
    for place, found in zip(maps, spread_tiles(tiles)):
        stack = jnp.concatenate([value[:, t * LANES : (t + 1) * LANES] for t in found], axis=0)
        parts.append(mm(place, stack).astype(BF16))
    return jnp.concatenate(parts, axis=1).reshape(blocks, ROWS, len(parts) * LANES)


def unfold_maps(slots, blocks, tiles):
    shape = (slots, blocks * ROWS)
    slot, lane = iota(shape, 0), iota(shape, 1)
    block = sixth(slot)
    maps = []
    for w, found in enumerate(spread_tiles(tiles)):
        places = []
        for t in found:
            row = slot - block * CAP + (t * CAP - w * ROWS)
            places.append(onehot((lane == block * ROWS + row) & (row >= 0) & (row < ROWS)))
        maps.append(jnp.concatenate(places, axis=0))
    return maps


def unfold(maps, value, slots, tiles):
    value = value.reshape(value.shape[0] * ROWS, value.shape[2])
    out = [None] * tiles
    for w, found in enumerate(spread_tiles(tiles)):
        got = mm(maps[w], value[:, w * LANES : (w + 1) * LANES])
        for p, t in enumerate(found):
            piece = got[p * slots : (p + 1) * slots]
            out[t] = piece if out[t] is None else out[t] + piece
    return jnp.concatenate(out, axis=1).astype(BF16)


def layer(
    n, m, tokens, picks, gates, w_gate, w_up, w_down, cotangent,
    mixed_out, dots_done, sel_out, back_grad,
    gate_v, up_v, down_v, send, recv, part, part_in, part_h, part_h_in, act_v, act_in, grad_v,
    grad_in, dot_v, dot_in, dot_sum, dot_back, ret, back, mixed_v, gg_v, sel_v,
    w_sem, dp_send, dp_recv, ex_send, ex_recv, out_sem,
):
    me = lax.axis_index("dp")
    mine = lax.axis_index("expert")
    tok, feat = tokens.shape
    tiles = feat // LANES
    top = picks.shape[0]
    slots = n * CAP
    hid_c = act_v.shape[1]
    wide = dot_v.shape[1]
    near = sorted(range(1, n), key=lambda o: -min(o, n - o))
    steps = [m // 2] + [o for o in range(1, m) if o != m // 2] if m > 1 else []

    def ring(index, step, size):
        return lax.rem(index + (step % size), size)

    def to_dp(phase, o, src, dst, step):
        copy = pltpu.make_async_remote_copy(
            src_ref=src, dst_ref=dst,
            send_sem=dp_send.at[phase, o], recv_sem=dp_recv.at[phase, o],
            device_id={"dp": ring(me, step, n)},
        )
        copy.start()
        return copy

    def to_expert(phase, o, src, dst):
        copy = pltpu.make_async_remote_copy(
            src_ref=src, dst_ref=dst,
            send_sem=ex_send.at[phase, o], recv_sem=ex_recv.at[phase, o],
            device_id={"expert": ring(mine, o, m)},
        )
        copy.start()
        return copy

    barrier = pltpu.get_barrier_semaphore()
    for o in range(1, n):
        pl.semaphore_signal(barrier, inc=1, device_id={"dp": ring(me, o, n)})
    for o in range(1, m):
        pl.semaphore_signal(barrier, inc=1, device_id={"expert": ring(mine, o, m)})

    loads = [
        pltpu.make_async_copy(src.at[0], dst, w_sem.at[i])
        for i, (src, dst) in enumerate(((w_gate, gate_v), (w_up, up_v), (w_down, down_v)))
    ]
    for load in loads:
        load.start()

    slot = iota((slots, tok), 0)
    offset = sixth(slot)
    place = slot - offset * CAP
    named = me + offset
    named = jnp.where(named >= n, named - n, named)
    picked = jnp.zeros((slots, tok), F32)
    gate_of = jnp.zeros((slots, tok), F32)
    for k in range(top):
        hit = picks[k : k + 1, :] == named
        picked = jnp.where(hit, 1.0, picked)
        gate_of = jnp.where(hit, gates[k : k + 1, :], gate_of)
    earlier = onehot(iota((tok, tok), 0) < iota((tok, tok), 1))
    rank = mm(picked.astype(BF16), earlier)
    chosen = (picked > 0.5) & (rank == place.astype(F32))
    sel = onehot(chosen)
    weight = jnp.where(chosen, gate_of, 0.0)
    folds = fold_maps(slots, n, tiles)
    send[0] = fold(folds, mm(sel, tokens[...]).astype(BF16), n)

    pl.semaphore_wait(barrier, n - 1 + m - 1)
    tok_out = [to_dp(0, o, send.at[0, o], recv.at[0, o], o) for o in near]
    slot_gate = jnp.sum(weight, axis=1, keepdims=True)
    send[1] = fold(folds, (mm(sel, cotangent[...]) * slot_gate).astype(BF16), n)
    cot_out = [to_dp(1, o, send.at[1, o], recv.at[1, o], o) for o in near]
    recv[0, 0] = send[0, 0]
    recv[1, 0] = send[1, 0]

    sel_v[...] = sel
    save_sel = pltpu.make_async_copy(sel_v, sel_out, out_sem.at[0])
    save_sel.start()
    unfolds = unfold_maps(slots, n, tiles)

    def columns(owner):
        return pl.ds(pl.multiple_of(owner * hid_c, LANES), hid_c)

    for copy in tok_out:
        copy.wait_recv()
    x_tok = unfold(unfolds, recv[0], slots, tiles)
    loads[0].wait()
    loads[1].wait()
    summing = []
    for o in steps:
        at = columns(ring(mine, o, m))
        part[o, :, :hid_c] = mm(x_tok, gate_v[:, at]).astype(BF16)
        part[o, :, hid_c:] = mm(x_tok, up_v[:, at]).astype(BF16)
        summing.append(to_expert(0, o, part.at[o], part_in.at[o]))
    here = columns(mine)
    gate_pre = mm(x_tok, gate_v[:, here])
    up_pre = mm(x_tok, up_v[:, here])

    for copy in cot_out:
        copy.wait_recv()
    x_cot = unfold(unfolds, recv[1], slots, tiles)
    loads[2].wait()
    summing_h = []
    for o in steps:
        part_h[o] = mm(x_cot, down_v[columns(ring(mine, o, m)), :], NT).astype(BF16)
        summing_h.append(to_expert(1, o, part_h.at[o], part_h_in.at[o]))
    grad_hidden = mm(x_cot, down_v[here, :], NT)

    for o, copy in zip(steps, summing):
        copy.wait_recv()
        gate_pre += part_in[o, :, :hid_c].astype(F32)
        up_pre += part_in[o, :, hid_c:].astype(F32)
    logistic = jax.nn.sigmoid(gate_pre)
    silu = gate_pre * logistic
    act = (silu * up_pre).astype(BF16)
    act_v[...] = act
    spread_act = [to_expert(2, o, act_v, act_in.at[o]) for o in steps]
    slope = up_pre * (logistic * (1.0 + gate_pre * (1.0 - logistic)))
    for o, copy in zip(steps, summing_h):
        copy.wait_recv()
        grad_hidden += part_h_in[o].astype(F32)
    grad_v[:, :hid_c] = (grad_hidden * slope).astype(BF16)
    grad_v[:, hid_c:] = (grad_hidden * silu).astype(BF16)
    spread_grad = [to_expert(3, o, grad_v, grad_in.at[o]) for o in steps]
    dots = jnp.sum(act.astype(F32) * grad_hidden, axis=1, keepdims=True)
    diag = iota((slots, wide), 0) == iota((slots, wide), 1)
    dots = jnp.sum(jnp.where(diag, dots, 0.0), axis=0, keepdims=True)
    dot_v[...] = dots
    spread_dot = [to_expert(4, o, dot_v, dot_in.at[o]) for o in steps]

    def grads(block, at):
        value = mm(block[:, :hid_c], gate_v[:, at], NT)
        return value + mm(block[:, hid_c:], up_v[:, at], NT)

    out = mm(act, down_v[here, :])
    for o, copy in reversed(list(zip(steps, spread_act))):
        copy.wait_recv()
        out += mm(act_in[o], down_v[columns(ring(mine, m - o, m)), :])
    ret[0] = fold(folds, out.astype(BF16), n)
    out_home = [to_dp(2, o, ret.at[0, o], back.at[o], n - o) for o in near]
    back[0] = ret[0, 0]
    for o, copy in zip(steps, spread_dot):
        copy.wait_recv()
        dots += dot_in[o]
    dot_sum[...] = dots
    dots_home = [to_dp(3, o, dot_sum, dot_back.at[o], n - o) for o in near]
    dot_back[0] = dots

    grad = grads(grad_v, here)
    for o, copy in reversed(list(zip(steps, spread_grad))):
        copy.wait_recv()
        grad += grads(grad_in.at[o], columns(ring(mine, m - o, m)))
    ret[1] = fold(folds, grad.astype(BF16), n)
    grad_home = [to_dp(4, o, ret.at[1, o], back_grad.at[o], n - o) for o in near]
    keep = pltpu.make_async_copy(ret.at[1, 0], back_grad.at[0], out_sem.at[1])
    keep.start()

    for copy in out_home:
        copy.wait_recv()
    y_out = unfold(unfolds, back[...], slots, tiles)
    weight_hi = weight.astype(BF16)
    weight_lo = (weight - weight_hi.astype(F32)).astype(BF16)
    mixed_v[...] = (mm(weight_hi, y_out, TN) + mm(weight_lo, y_out, TN)).astype(BF16)
    save_mixed = pltpu.make_async_copy(mixed_v, mixed_out, out_sem.at[2])
    save_mixed.start()
    for copy in dots_home:
        copy.wait_recv()
    lane = sixth(iota((1, wide), 1))
    dots = jnp.zeros((1, wide), F32)
    for o in range(n):
        dots = jnp.where(lane == o, dot_back[o], dots)
    dots = jnp.sum(jnp.where(diag, dots, 0.0), axis=1, keepdims=True)
    value = jnp.where(chosen, dots, 0.0)
    for k in range(top):
        hit = picks[k : k + 1, :] == named
        gg_v[k : k + 1, :] = (
            jnp.sum(jnp.where(hit, value, 0.0), axis=0, keepdims=True) / gates[k : k + 1, :]
        )
    save_gg = pltpu.make_async_copy(gg_v, dots_done, out_sem.at[3])
    save_gg.start()

    for copy in grad_home:
        copy.wait_recv()
    for copy in (save_sel, keep, save_mixed, save_gg):
        copy.wait()
    for copy in (
        tok_out + cot_out + summing + summing_h + spread_act + spread_grad + spread_dot
        + out_home + dots_home + grad_home
    ):
        copy.wait_send()


def finish(mixed, dots, sel, back, mixed_out, grad_tokens, grad_gates):
    blocks = back.shape[0]
    slots = sel.shape[0]
    tiles = mixed.shape[1] // LANES
    y_grad = unfold(unfold_maps(slots, blocks, tiles), back[...], slots, tiles)
    grad_tokens[...] = mm(sel[...], y_grad, TN).astype(BF16)
    mixed_out[...] = mixed[...]
    grad_gates[...] = dots[...]


def shards(tokens, picks, gates, w_gate, w_up, w_down, cotangent):
    n = lax.axis_size("dp")
    m = lax.axis_size("expert")
    tok, feat = tokens.shape
    top = picks.shape[1]
    hidden = w_gate.shape[2]
    slots = n * CAP
    share = hidden // m
    hid_c = -(-share // LANES) * LANES
    if hid_c != share:
        fill = hid_c - share
        w_gate, w_up = (
            jnp.pad(w.reshape(1, feat, m, share), ((0, 0), (0, 0), (0, 0), (0, fill))).reshape(
                1, feat, m * hid_c
            )
            for w in (w_gate, w_up)
        )
        w_down = jnp.pad(
            w_down.reshape(1, m, share, feat), ((0, 0), (0, 0), (0, fill), (0, 0))
        ).reshape(1, m * hid_c, feat)
    wide = -(-slots // LANES) * LANES
    block = LANES * len(spread_tiles(feat // LANES))
    vmem = pl.BlockSpec(memory_space=pltpu.VMEM)
    hbm = pl.BlockSpec(memory_space=pl.ANY)
    dma = pltpu.SemaphoreType.DMA
    array = jax.ShapeDtypeStruct
    mixed, dots, sel, back = pl.pallas_call(
        functools.partial(layer, n, m),
        out_shape=(
            array((tok, feat), BF16),
            array((top, tok), F32),
            array((slots, tok), BF16),
            array((n, ROWS, block), BF16),
        ),
        in_specs=[vmem, vmem, vmem, hbm, hbm, hbm, vmem],
        out_specs=(hbm, hbm, hbm, hbm),
        scratch_shapes=[
            pltpu.VMEM((feat, m * hid_c), BF16),
            pltpu.VMEM((feat, m * hid_c), BF16),
            pltpu.VMEM((m * hid_c, feat), BF16),
            pltpu.VMEM((2, n, ROWS, block), BF16),
            pltpu.VMEM((2, n, ROWS, block), BF16),
            pltpu.VMEM((m, slots, 2 * hid_c), BF16),
            pltpu.VMEM((m, slots, 2 * hid_c), BF16),
            pltpu.VMEM((m, slots, hid_c), BF16),
            pltpu.VMEM((m, slots, hid_c), BF16),
            pltpu.VMEM((slots, hid_c), BF16),
            pltpu.VMEM((m, slots, hid_c), BF16),
            pltpu.VMEM((slots, 2 * hid_c), BF16),
            pltpu.VMEM((m, slots, 2 * hid_c), BF16),
            pltpu.VMEM((1, wide), F32),
            pltpu.VMEM((m, 1, wide), F32),
            pltpu.VMEM((1, wide), F32),
            pltpu.VMEM((n, 1, wide), F32),
            pltpu.VMEM((2, n, ROWS, block), BF16),
            pltpu.VMEM((n, ROWS, block), BF16),
            pltpu.VMEM((tok, feat), BF16),
            pltpu.VMEM((top, tok), F32),
            pltpu.VMEM((slots, tok), BF16),
            dma((3,)),
            dma((5, n)),
            dma((5, n)),
            dma((5, m)),
            dma((5, m)),
            dma((4,)),
        ],
        compiler_params=pltpu.CompilerParams(
            collective_id=0, has_side_effects=True, vmem_limit_bytes=56 * 1024 * 1024
        ),
    )(tokens, picks.T, gates.T, w_gate, w_up, w_down, cotangent)
    mixed, grad_tokens, dots = pl.pallas_call(
        finish,
        out_shape=(
            array((tok, feat), BF16),
            array((tok, feat), BF16),
            array((top, tok), F32),
        ),
        in_specs=[vmem] * 4,
        out_specs=(vmem, vmem, vmem),
    )(mixed, dots, sel, back)
    return mixed, grad_tokens, dots.T


def solution(mesh):
    placed = (
        P("dp", "expert"),
        P("dp", None),
        P("dp", None),
        P("dp", "expert", None),
        P("dp", "expert", None),
        P("dp", None, "expert"),
        P("dp", "expert"),
    )
    return jax.shard_map(
        shards,
        mesh=mesh,
        in_specs=placed,
        out_specs=(P("dp", "expert"), P("dp", "expert"), P("dp", None)),
        check_vma=False,
    )
```

```python
import functools

import jax
import jax.numpy as jnp
from jax import lax
from jax.experimental import pallas as pl
from jax.experimental.pallas import tpu as pltpu
from jax.sharding import PartitionSpec as P

CAP = 6
ROWS = 16
LANES = 128
BF16 = jnp.bfloat16
F32 = jnp.float32
NN = (((1,), (0,)), ((), ()))
NT = (((1,), (1,)), ((), ()))
TN = (((0,), (0,)), ((), ()))


def mm(a, b, dims=NN):
    return lax.dot_general(a, b, dims, preferred_element_type=F32)


def iota(shape, dim):
    return lax.broadcasted_iota(jnp.int32, shape, dim)


def onehot(mask):
    return jnp.where(mask, 1.0, 0.0).astype(BF16)


def spread_tiles(tiles):
    wide = -(-tiles * CAP // ROWS)
    return [
        sorted({i // CAP for i in range(w * ROWS, min((w + 1) * ROWS, tiles * CAP))})
        for w in range(wide)
    ]


def sixth(value):
    return (value * 10923) >> 16


def fold_maps(slots, blocks, tiles):
    maps = []
    for w, found in enumerate(spread_tiles(tiles)):
        shape = (blocks * ROWS, len(found) * slots)
        row, lane = iota(shape, 0), iota(shape, 1)
        number = (row & (ROWS - 1)) + w * ROWS
        tile = sixth(number)
        target = (tile - found[0]) * slots + (row >> 4) * CAP + number - tile * CAP
        maps.append(onehot((lane == target) & (number < tiles * CAP)))
    return maps


def fold(maps, value, blocks):
    tiles = value.shape[1] // LANES
    parts = []
    for place, found in zip(maps, spread_tiles(tiles)):
        stack = jnp.concatenate([value[:, t * LANES : (t + 1) * LANES] for t in found], axis=0)
        parts.append(mm(place, stack).astype(BF16))
    return jnp.concatenate(parts, axis=1).reshape(blocks, ROWS, len(parts) * LANES)


def unfold_maps(slots, blocks, tiles):
    shape = (slots, blocks * ROWS)
    slot, lane = iota(shape, 0), iota(shape, 1)
    block = sixth(slot)
    maps = []
    for w, found in enumerate(spread_tiles(tiles)):
        places = []
        for t in found:
            row = slot - block * CAP + (t * CAP - w * ROWS)
            places.append(onehot((lane == block * ROWS + row) & (row >= 0) & (row < ROWS)))
        maps.append(jnp.concatenate(places, axis=0))
    return maps


def unfold(maps, value, slots, tiles):
    value = value.reshape(value.shape[0] * ROWS, value.shape[2])
    out = [None] * tiles
    for w, found in enumerate(spread_tiles(tiles)):
        got = mm(maps[w], value[:, w * LANES : (w + 1) * LANES])
        for p, t in enumerate(found):
            piece = got[p * slots : (p + 1) * slots]
            out[t] = piece if out[t] is None else out[t] + piece
    return jnp.concatenate(out, axis=1).astype(BF16)


def layer(
    n, m, tokens_in, picks_in, gates_in, w_gate, w_up, w_down, cotangent_in,
    mixed_out, dots_done, sel_out, back_grad,
    tokens, picks, gates, cotangent, cot_slot, gu_v, down_v, send, recv, part, part_in, part_h,
    part_h_in, act_v, act_in, grad_v, grad_in, dot_v, dot_in, ret, back, mixed_v, gg_v, sel_v,
    in_sem, w_sem, dp_send, dp_recv, ex_send, ex_recv, out_sem,
):
    me = lax.axis_index("dp")
    mine = lax.axis_index("expert")
    tok, feat = tokens.shape
    tiles = feat // LANES
    top = picks.shape[0]
    slots = n * CAP
    hid_c = act_v.shape[1]
    wide = dot_v.shape[1]
    near = sorted(range(1, n), key=lambda o: -min(o, n - o))
    steps = [m // 2] + [o for o in range(1, m) if o != m // 2] if m > 1 else []

    def ring(index, step, size):
        return lax.rem(index + (step % size), size)

    def to_dp(phase, o, src, dst, step):
        copy = pltpu.make_async_remote_copy(
            src_ref=src, dst_ref=dst,
            send_sem=dp_send.at[phase, o], recv_sem=dp_recv.at[phase, o],
            device_id={"dp": ring(me, step, n)},
        )
        copy.start()
        return copy

    def to_expert(phase, o, src, dst):
        copy = pltpu.make_async_remote_copy(
            src_ref=src, dst_ref=dst,
            send_sem=ex_send.at[phase, o], recv_sem=ex_recv.at[phase, o],
            device_id={"expert": ring(mine, o, m)},
        )
        copy.start()
        return copy

    def columns(owner, width):
        return pl.ds(pl.multiple_of(owner * width, LANES), width)

    arrive = [
        pltpu.make_async_copy(src, dst, in_sem.at[i])
        for i, (src, dst) in enumerate(
            ((picks_in, picks), (gates_in, gates), (tokens_in, tokens), (cotangent_in, cotangent))
        )
    ]
    for copy in arrive:
        copy.start()
    barrier = pltpu.get_barrier_semaphore()
    for o in range(1, n):
        pl.semaphore_signal(barrier, inc=1, device_id={"dp": ring(me, o, n)})
    for o in range(1, m):
        pl.semaphore_signal(barrier, inc=1, device_id={"expert": ring(mine, o, m)})

    loads = {}
    for o in steps + [0]:
        owner = ring(mine, o, m)
        for i, src in enumerate((w_gate, w_up)):
            at = pl.ds(pl.multiple_of((2 * owner + i) * hid_c, LANES), hid_c)
            loads[i, o] = pltpu.make_async_copy(
                src.at[0, :, columns(owner, hid_c)], gu_v.at[:, at], w_sem.at[i, o]
            )
            loads[i, o].start()
    for o in steps + [0]:
        rows = columns(ring(mine, o, m), hid_c)
        loads[2, o] = pltpu.make_async_copy(w_down.at[0, rows, :], down_v.at[rows, :], w_sem.at[2, o])
        loads[2, o].start()
    for copy in arrive[:2]:
        copy.wait()

    slot = iota((slots, tok), 0)
    offset = sixth(slot)
    place = slot - offset * CAP
    named = me + offset
    named = jnp.where(named >= n, named - n, named)
    picked = jnp.zeros((slots, tok), F32)
    gate_of = jnp.zeros((slots, tok), F32)
    for k in range(top):
        hit = picks[k : k + 1, :] == named
        picked = jnp.where(hit, 1.0, picked)
        gate_of = jnp.where(hit, gates[k : k + 1, :], gate_of)
    earlier = onehot(iota((tok, tok), 0) < iota((tok, tok), 1))
    rank = mm(picked.astype(BF16), earlier)
    chosen = (picked > 0.5) & (rank == place.astype(F32))
    sel = onehot(chosen)
    weight = jnp.where(chosen, gate_of, 0.0)
    folds = fold_maps(slots, n, tiles)
    arrive[2].wait()
    send[0] = fold(folds, mm(sel, tokens[...]).astype(BF16), n)

    pl.semaphore_wait(barrier, n - 1 + m - 1)
    tok_out = [to_dp(0, o, send.at[0, o], recv.at[0, o], o) for o in near]
    slot_gate = jnp.sum(weight, axis=1, keepdims=True)
    arrive[3].wait()
    chosen_cot = mm(sel, cotangent[...])
    send[1] = fold(folds, (chosen_cot * slot_gate).astype(BF16), n)
    cot_out = [to_dp(1, o, send.at[1, o], recv.at[1, o], o) for o in near]
    recv[0, 0] = send[0, 0]
    recv[1, 0] = send[1, 0]
    cot_slot[...] = chosen_cot.astype(BF16)

    sel_v[...] = sel
    save_sel = pltpu.make_async_copy(sel_v, sel_out, out_sem.at[0])
    save_sel.start()
    unfolds = unfold_maps(slots, n, tiles)

    for copy in tok_out:
        copy.wait_recv()
    x_tok = unfold(unfolds, recv[0], slots, tiles)
    summing = []
    for o in steps:
        loads[0, o].wait()
        loads[1, o].wait()
        part[o] = mm(x_tok, gu_v[:, columns(ring(mine, o, m), 2 * hid_c)]).astype(BF16)
        summing.append(to_expert(0, o, part.at[o], part_in.at[o]))
    loads[0, 0].wait()
    loads[1, 0].wait()
    both = mm(x_tok, gu_v[:, columns(mine, 2 * hid_c)])

    for copy in cot_out:
        copy.wait_recv()
    x_cot = unfold(unfolds, recv[1], slots, tiles)
    summing_h = []
    for o in steps:
        loads[2, o].wait()
        part_h[o] = mm(x_cot, down_v[columns(ring(mine, o, m), hid_c), :], NT).astype(BF16)
        summing_h.append(to_expert(1, o, part_h.at[o], part_h_in.at[o]))
    loads[2, 0].wait()
    grad_hidden = mm(x_cot, down_v[columns(mine, hid_c), :], NT)

    for o, copy in zip(steps, summing):
        copy.wait_recv()
        both += part_in[o].astype(F32)
    gate_pre = both[:, :hid_c]
    up_pre = both[:, hid_c:]
    logistic = jax.nn.sigmoid(gate_pre)
    silu = gate_pre * logistic
    act = (silu * up_pre).astype(BF16)
    act_v[...] = act
    spread_act = [to_expert(2, o, act_v, act_in.at[o]) for o in steps]
    slope = up_pre * (logistic * (1.0 + gate_pre * (1.0 - logistic)))
    for o, copy in zip(steps, summing_h):
        copy.wait_recv()
        grad_hidden += part_h_in[o].astype(F32)
    grad_v[:, :hid_c] = (grad_hidden * slope).astype(BF16)
    grad_v[:, hid_c:] = (grad_hidden * silu).astype(BF16)
    spread_grad = [to_expert(3, o, grad_v, grad_in.at[o]) for o in steps]
    out = mm(act, down_v[columns(mine, hid_c), :])
    for o, copy in reversed(list(zip(steps, spread_act))):
        copy.wait_recv()
        out += mm(act_in[o], down_v[columns(ring(mine, m - o, m), hid_c), :])
    ret[0] = fold(folds, out.astype(BF16), n)
    out_home = [to_dp(2, o, ret.at[0, o], back.at[o], n - o) for o in near]
    back[0] = ret[0, 0]
    grad = mm(grad_v[...], gu_v[:, columns(mine, 2 * hid_c)], NT)
    for o, copy in reversed(list(zip(steps, spread_grad))):
        copy.wait_recv()
        grad += mm(grad_in[o], gu_v[:, columns(ring(mine, m - o, m), 2 * hid_c)], NT)
    ret[1] = fold(folds, grad.astype(BF16), n)
    grad_home = [to_dp(3, o, ret.at[1, o], back_grad.at[o], n - o) for o in near]
    keep = pltpu.make_async_copy(ret.at[1, 0], back_grad.at[0], out_sem.at[1])
    keep.start()

    for copy in out_home:
        copy.wait_recv()
    y_out = unfold(unfolds, back[...], slots, tiles)
    dots = cot_slot[...].astype(F32) * y_out.astype(F32)
    dots = jnp.sum(dots, axis=1, keepdims=True)
    diag = iota((slots, wide), 0) == iota((slots, wide), 1)
    dots = jnp.sum(jnp.where(diag, dots, 0.0), axis=0, keepdims=True)
    dot_v[...] = dots
    spread_dot = [to_expert(4, o, dot_v, dot_in.at[o]) for o in steps]
    weight_hi = weight.astype(BF16)
    weight_lo = (weight - weight_hi.astype(F32)).astype(BF16)
    mixed_v[...] = (mm(weight_hi, y_out, TN) + mm(weight_lo, y_out, TN)).astype(BF16)
    save_mixed = pltpu.make_async_copy(mixed_v, mixed_out, out_sem.at[2])
    save_mixed.start()
    for copy in tok_out + cot_out + summing + summing_h + spread_act + spread_grad + out_home:
        copy.wait_send()
    for o, copy in zip(steps, spread_dot):
        copy.wait_recv()
        dots += dot_in[o]
    dots = jnp.sum(jnp.where(diag, dots, 0.0), axis=1, keepdims=True)
    value = jnp.where(chosen, dots, 0.0)
    for k in range(top):
        hit = picks[k : k + 1, :] == named
        gg_v[k : k + 1, :] = jnp.sum(jnp.where(hit, value, 0.0), axis=0, keepdims=True)
    save_gg = pltpu.make_async_copy(gg_v, dots_done, out_sem.at[3])
    save_gg.start()

    for copy in (save_sel, keep, save_mixed):
        copy.wait()
    for copy in spread_dot + grad_home:
        copy.wait_send()
    for copy in grad_home:
        copy.wait_recv()
    save_gg.wait()


def finish(mixed, dots, sel, back, mixed_out, grad_tokens, grad_gates):
    blocks = back.shape[0]
    slots = sel.shape[0]
    tiles = mixed.shape[1] // LANES
    y_grad = unfold(unfold_maps(slots, blocks, tiles), back[...], slots, tiles)
    grad_tokens[...] = mm(sel[...], y_grad, TN).astype(BF16)
    mixed_out[...] = mixed[...]
    grad_gates[...] = dots[...]


def shards(tokens, picks, gates, w_gate, w_up, w_down, cotangent):
    n = lax.axis_size("dp")
    m = lax.axis_size("expert")
    tok, feat = tokens.shape
    top = picks.shape[1]
    hidden = w_gate.shape[2]
    slots = n * CAP
    share = hidden // m
    hid_c = -(-share // LANES) * LANES
    if hid_c != share:
        fill = hid_c - share
        w_gate, w_up = (
            jnp.pad(w.reshape(1, feat, m, share), ((0, 0), (0, 0), (0, 0), (0, fill))).reshape(
                1, feat, m * hid_c
            )
            for w in (w_gate, w_up)
        )
        w_down = jnp.pad(
            w_down.reshape(1, m, share, feat), ((0, 0), (0, 0), (0, fill), (0, 0))
        ).reshape(1, m * hid_c, feat)
    wide = -(-slots // LANES) * LANES
    block = LANES * len(spread_tiles(feat // LANES))
    vmem = pl.BlockSpec(memory_space=pltpu.VMEM)
    hbm = pl.BlockSpec(memory_space=pl.ANY)
    dma = pltpu.SemaphoreType.DMA
    array = jax.ShapeDtypeStruct
    mixed, dots, sel, back = pl.pallas_call(
        functools.partial(layer, n, m),
        out_shape=(
            array((tok, feat), BF16),
            array((top, tok), F32),
            array((slots, tok), BF16),
            array((n, ROWS, block), BF16),
        ),
        in_specs=[hbm] * 7,
        out_specs=(hbm, hbm, hbm, hbm),
        scratch_shapes=[
            pltpu.VMEM((tok, feat), BF16),
            pltpu.VMEM((top, tok), jnp.int32),
            pltpu.VMEM((top, tok), F32),
            pltpu.VMEM((tok, feat), BF16),
            pltpu.VMEM((slots, feat), BF16),
            pltpu.VMEM((feat, 2 * m * hid_c), BF16),
            pltpu.VMEM((m * hid_c, feat), BF16),
            pltpu.VMEM((2, n, ROWS, block), BF16),
            pltpu.VMEM((2, n, ROWS, block), BF16),
            pltpu.VMEM((m, slots, 2 * hid_c), BF16),
            pltpu.VMEM((m, slots, 2 * hid_c), BF16),
            pltpu.VMEM((m, slots, hid_c), BF16),
            pltpu.VMEM((m, slots, hid_c), BF16),
            pltpu.VMEM((slots, hid_c), BF16),
            pltpu.VMEM((m, slots, hid_c), BF16),
            pltpu.VMEM((slots, 2 * hid_c), BF16),
            pltpu.VMEM((m, slots, 2 * hid_c), BF16),
            pltpu.VMEM((1, wide), F32),
            pltpu.VMEM((m, 1, wide), F32),
            pltpu.VMEM((2, n, ROWS, block), BF16),
            pltpu.VMEM((n, ROWS, block), BF16),
            pltpu.VMEM((tok, feat), BF16),
            pltpu.VMEM((top, tok), F32),
            pltpu.VMEM((slots, tok), BF16),
            dma((4,)),
            dma((3, m)),
            dma((4, n)),
            dma((4, n)),
            dma((5, m)),
            dma((5, m)),
            dma((4,)),
        ],
        compiler_params=pltpu.CompilerParams(
            collective_id=0, has_side_effects=True, vmem_limit_bytes=56 * 1024 * 1024
        ),
    )(tokens, picks.T, gates.T, w_gate, w_up, w_down, cotangent)
    mixed, grad_tokens, dots = pl.pallas_call(
        finish,
        out_shape=(
            array((tok, feat), BF16),
            array((tok, feat), BF16),
            array((top, tok), F32),
        ),
        in_specs=[vmem] * 4,
        out_specs=(vmem, vmem, vmem),
    )(mixed, dots, sel, back)
    return mixed, grad_tokens, dots.T


def solution(mesh):
    placed = (
        P("dp", "expert"),
        P("dp", None),
        P("dp", None),
        P("dp", "expert", None),
        P("dp", "expert", None),
        P("dp", None, "expert"),
        P("dp", "expert"),
    )
    return jax.shard_map(
        shards,
        mesh=mesh,
        in_specs=placed,
        out_specs=(P("dp", "expert"), P("dp", "expert"), P("dp", None)),
        check_vma=False,
    )
```

```python
import functools

import jax
import jax.numpy as jnp
from jax import lax
from jax.experimental import pallas as pl
from jax.experimental.pallas import tpu as pltpu
from jax.sharding import PartitionSpec as P

CAP = 6
ROWS = 16
LANES = 128
BF16 = jnp.bfloat16
F32 = jnp.float32
NN = (((1,), (0,)), ((), ()))
NT = (((1,), (1,)), ((), ()))
TN = (((0,), (0,)), ((), ()))


def mm(a, b, dims=NN):
    return lax.dot_general(a, b, dims, preferred_element_type=F32)


def iota(shape, dim):
    return lax.broadcasted_iota(jnp.int32, shape, dim)


def onehot(mask):
    return jnp.where(mask, 1.0, 0.0).astype(BF16)


def spread_tiles(tiles):
    wide = -(-tiles * CAP // ROWS)
    return [
        sorted({i // CAP for i in range(w * ROWS, min((w + 1) * ROWS, tiles * CAP))})
        for w in range(wide)
    ]


def sixth(value):
    return (value * 10923) >> 16


def fold_maps(slots, blocks, tiles):
    maps = []
    for w, found in enumerate(spread_tiles(tiles)):
        shape = (blocks * ROWS, len(found) * slots)
        row, lane = iota(shape, 0), iota(shape, 1)
        number = (row & (ROWS - 1)) + w * ROWS
        tile = sixth(number)
        target = (tile - found[0]) * slots + (row >> 4) * CAP + number - tile * CAP
        maps.append(onehot((lane == target) & (number < tiles * CAP)))
    return maps


def cut(value):
    return [value[:, at : at + LANES] for at in range(0, value.shape[1], LANES)]


def fold_one(place, tiles, blocks):
    return mm(place, jnp.concatenate(tiles, axis=0)).astype(BF16).reshape(blocks, ROWS, LANES)


def fold(maps, value, blocks):
    value = cut(value)
    parts = [
        fold_one(place, [value[t] for t in found], blocks)
        for place, found in zip(maps, spread_tiles(len(value)))
    ]
    return jnp.concatenate(parts, axis=2)


def unfold_maps(slots, blocks, tiles):
    shape = (slots, blocks * ROWS)
    slot, lane = iota(shape, 0), iota(shape, 1)
    block = sixth(slot)
    maps = []
    for w, found in enumerate(spread_tiles(tiles)):
        places = []
        for t in found:
            row = slot - block * CAP + (t * CAP - w * ROWS)
            places.append(onehot((lane == block * ROWS + row) & (row >= 0) & (row < ROWS)))
        maps.append(jnp.concatenate(places, axis=0))
    return maps


def unfold(maps, value, slots, tiles):
    out = [None] * tiles
    for w, found in enumerate(spread_tiles(tiles)):
        part = value[:, :, w * LANES : (w + 1) * LANES] if len(value.shape) == 3 else value[w]
        got = mm(maps[w], part.reshape(part.shape[0] * ROWS, LANES))
        for p, t in enumerate(found):
            piece = got[p * slots : (p + 1) * slots]
            out[t] = piece if out[t] is None else out[t] + piece
    return jnp.concatenate(out, axis=1).astype(BF16)


def layer(
    n, m, tokens_in, picks_in, gates_in, w_gate, w_up, w_down, cotangent_in,
    mixed_out, dots_done, sel_out, back_grad,
    tokens, picks, gates, cotangent, cot_slot, gu_v, down_v, send, recv, part, part_in, part_h,
    part_h_in, act_v, act_in, grad_v, grad_in, dot_v, dot_in, ret, ret_grad, back, mixed_v, gg_v,
    sel_v,
    in_sem, w_sem, dp_send, dp_recv, ex_send, ex_recv, out_sem,
):
    me = lax.axis_index("dp")
    mine = lax.axis_index("expert")
    tok, feat = tokens.shape
    tiles = feat // LANES
    top = picks.shape[0]
    slots = n * CAP
    hid_c = act_v.shape[1]
    wide = dot_v.shape[1]
    near = sorted(range(1, n), key=lambda o: -min(o, n - o))
    steps = [m // 2] + [o for o in range(1, m) if o != m // 2] if m > 1 else []

    def ring(index, step, size):
        return lax.rem(index + (step % size), size)

    def to_dp(phase, o, src, dst, step):
        copy = pltpu.make_async_remote_copy(
            src_ref=src, dst_ref=dst,
            send_sem=dp_send.at[phase, o], recv_sem=dp_recv.at[phase, o],
            device_id={"dp": ring(me, step, n)},
        )
        copy.start()
        return copy

    def to_expert(phase, o, src, dst):
        copy = pltpu.make_async_remote_copy(
            src_ref=src, dst_ref=dst,
            send_sem=ex_send.at[phase, o], recv_sem=ex_recv.at[phase, o],
            device_id={"expert": ring(mine, o, m)},
        )
        copy.start()
        return copy

    def columns(owner, width):
        return pl.ds(pl.multiple_of(owner * width, LANES), width)

    arrive = [
        pltpu.make_async_copy(src, dst, in_sem.at[i])
        for i, (src, dst) in enumerate(
            ((picks_in, picks), (gates_in, gates), (tokens_in, tokens), (cotangent_in, cotangent))
        )
    ]
    for copy in arrive:
        copy.start()
    barrier = pltpu.get_barrier_semaphore()
    for o in range(1, n):
        pl.semaphore_signal(barrier, inc=1, device_id={"dp": ring(me, o, n)})
    for o in range(1, m):
        pl.semaphore_signal(barrier, inc=1, device_id={"expert": ring(mine, o, m)})

    loads = {}
    for o in steps + [0]:
        owner = ring(mine, o, m)
        for i, src in enumerate((w_gate, w_up)):
            at = pl.ds(pl.multiple_of((2 * owner + i) * hid_c, LANES), hid_c)
            loads[i, o] = pltpu.make_async_copy(
                src.at[0, :, columns(owner, hid_c)], gu_v.at[:, at], w_sem.at[i, o]
            )
            loads[i, o].start()
    for o in steps + [0]:
        rows = columns(ring(mine, o, m), hid_c)
        loads[2, o] = pltpu.make_async_copy(w_down.at[0, rows, :], down_v.at[rows, :], w_sem.at[2, o])
        loads[2, o].start()
    for copy in arrive[:2]:
        copy.wait()

    slot = iota((slots, tok), 0)
    offset = sixth(slot)
    place = slot - offset * CAP
    named = me + offset
    named = jnp.where(named >= n, named - n, named)
    picked = jnp.zeros((slots, tok), F32)
    gate_of = jnp.zeros((slots, tok), F32)
    for k in range(top):
        hit = picks[k : k + 1, :] == named
        picked = jnp.where(hit, 1.0, picked)
        gate_of = jnp.where(hit, gates[k : k + 1, :], gate_of)
    earlier = onehot(iota((tok, tok), 0) < iota((tok, tok), 1))
    rank = mm(picked.astype(BF16), earlier)
    chosen = (picked > 0.5) & (rank == place.astype(F32))
    sel = onehot(chosen)
    weight = jnp.where(chosen, gate_of, 0.0)
    folds = fold_maps(slots, n, tiles)
    arrive[2].wait()
    send[0] = fold(folds, mm(sel, tokens[...]).astype(BF16), n)

    pl.semaphore_wait(barrier, n - 1 + m - 1)
    tok_out = [to_dp(0, o, send.at[0, o], recv.at[0, o], o) for o in near]
    slot_gate = jnp.sum(weight, axis=1, keepdims=True)
    arrive[3].wait()
    chosen_cot = mm(sel, cotangent[...])
    send[1] = fold(folds, (chosen_cot * slot_gate).astype(BF16), n)
    cot_out = [to_dp(1, o, send.at[1, o], recv.at[1, o], o) for o in near]
    recv[0, 0] = send[0, 0]
    recv[1, 0] = send[1, 0]
    cot_slot[...] = chosen_cot.astype(BF16)

    sel_v[...] = sel
    save_sel = pltpu.make_async_copy(sel_v, sel_out, out_sem.at[0])
    save_sel.start()
    unfolds = unfold_maps(slots, n, tiles)

    for copy in tok_out:
        copy.wait_recv()
    x_tok = unfold(unfolds, recv[0], slots, tiles)
    summing = []
    for o in steps:
        loads[0, o].wait()
        loads[1, o].wait()
        part[o] = mm(x_tok, gu_v[:, columns(ring(mine, o, m), 2 * hid_c)]).astype(BF16)
        summing.append(to_expert(0, o, part.at[o], part_in.at[o]))
    loads[0, 0].wait()
    loads[1, 0].wait()
    both = mm(x_tok, gu_v[:, columns(mine, 2 * hid_c)])

    for copy in cot_out:
        copy.wait_recv()
    x_cot = unfold(unfolds, recv[1], slots, tiles)
    summing_h = []
    for o in steps:
        loads[2, o].wait()
        part_h[o] = mm(x_cot, down_v[columns(ring(mine, o, m), hid_c), :], NT).astype(BF16)
        summing_h.append(to_expert(1, o, part_h.at[o], part_h_in.at[o]))
    loads[2, 0].wait()
    grad_hidden = mm(x_cot, down_v[columns(mine, hid_c), :], NT)

    for o, copy in zip(steps, summing):
        copy.wait_recv()
        both += part_in[o].astype(F32)
    gate_pre = both[:, :hid_c]
    up_pre = both[:, hid_c:]
    logistic = jax.nn.sigmoid(gate_pre)
    silu = gate_pre * logistic
    act = (silu * up_pre).astype(BF16)
    act_v[...] = act
    spread_act = [to_expert(2, o, act_v, act_in.at[o]) for o in steps]
    slope = up_pre * (logistic * (1.0 + gate_pre * (1.0 - logistic)))
    for o, copy in zip(steps, summing_h):
        copy.wait_recv()
        grad_hidden += part_h_in[o].astype(F32)
    grad_v[:, :hid_c] = (grad_hidden * slope).astype(BF16)
    grad_v[:, hid_c:] = (grad_hidden * silu).astype(BF16)
    spread_grad = [to_expert(3, o, grad_v, grad_in.at[o]) for o in steps]
    out = mm(act, down_v[columns(mine, hid_c), :])
    own_grad = mm(grad_v[...], gu_v[:, columns(mine, 2 * hid_c)], NT)
    for o, copy in reversed(list(zip(steps, spread_act))):
        copy.wait_recv()
        out += mm(act_in[o], down_v[columns(ring(mine, m - o, m), hid_c), :])
    ret[...] = fold(folds, out.astype(BF16), n)
    out_home = [to_dp(2, o, ret.at[o], back.at[o], n - o) for o in near]
    back[0] = ret[0]
    for copy in spread_grad:
        copy.wait_recv()
    grad = []
    grad_home = []
    keep = []
    for w, found in enumerate(spread_tiles(tiles)):
        rows = slice(len(grad) * LANES, (found[-1] + 1) * LANES)
        piece = own_grad[:, rows]
        for o in steps:
            at = columns(ring(mine, m - o, m), 2 * hid_c)
            piece += mm(grad_in[o], gu_v[rows, at], NT)
        grad += cut(piece.astype(BF16))
        ret_grad[w] = fold_one(folds[w], [grad[t] for t in found], n)
        for o in near:
            grad_home.append(to_dp(3 + w, o, ret_grad.at[w, o], back_grad.at[w, o], n - o))
        keep.append(pltpu.make_async_copy(ret_grad.at[w, 0], back_grad.at[w, 0], out_sem.at[3 + w]))
        keep[w].start()

    for copy in out_home:
        copy.wait_recv()
    y_out = unfold(unfolds, back[...], slots, tiles)
    dots = cot_slot[...].astype(F32) * y_out.astype(F32)
    dots = jnp.sum(dots, axis=1, keepdims=True)
    diag = iota((slots, wide), 0) == iota((slots, wide), 1)
    dots = jnp.sum(jnp.where(diag, dots, 0.0), axis=0, keepdims=True)
    dot_v[...] = dots
    spread_dot = [to_expert(4, o, dot_v, dot_in.at[o]) for o in steps]
    weight_hi = weight.astype(BF16)
    weight_lo = (weight - weight_hi.astype(F32)).astype(BF16)
    mixed_v[...] = (mm(weight_hi, y_out, TN) + mm(weight_lo, y_out, TN)).astype(BF16)
    save_mixed = pltpu.make_async_copy(mixed_v, mixed_out, out_sem.at[1])
    save_mixed.start()
    for copy in tok_out + cot_out + summing + summing_h + spread_act + spread_grad + out_home:
        copy.wait_send()
    for o, copy in zip(steps, spread_dot):
        copy.wait_recv()
        dots += dot_in[o]
    dots = jnp.sum(jnp.where(diag, dots, 0.0), axis=1, keepdims=True)
    value = jnp.where(chosen, dots, 0.0)
    for k in range(top):
        hit = picks[k : k + 1, :] == named
        gg_v[k : k + 1, :] = jnp.sum(jnp.where(hit, value, 0.0), axis=0, keepdims=True)
    save_gg = pltpu.make_async_copy(gg_v, dots_done, out_sem.at[2])
    save_gg.start()

    for copy in [save_sel, save_mixed] + keep:
        copy.wait()
    for copy in spread_dot + grad_home:
        copy.wait_send()
    for copy in grad_home:
        copy.wait_recv()
    save_gg.wait()


def finish(mixed, dots, sel, back, mixed_out, grad_tokens, grad_gates):
    blocks = back.shape[1]
    slots = sel.shape[0]
    tiles = mixed.shape[1] // LANES
    y_grad = unfold(unfold_maps(slots, blocks, tiles), back[...], slots, tiles)
    grad_tokens[...] = mm(sel[...], y_grad, TN).astype(BF16)
    mixed_out[...] = mixed[...]
    grad_gates[...] = dots[...]


def shards(tokens, picks, gates, w_gate, w_up, w_down, cotangent):
    n = lax.axis_size("dp")
    m = lax.axis_size("expert")
    tok, feat = tokens.shape
    top = picks.shape[1]
    hidden = w_gate.shape[2]
    slots = n * CAP
    share = hidden // m
    hid_c = -(-share // LANES) * LANES
    if hid_c != share:
        fill = hid_c - share
        w_gate, w_up = (
            jnp.pad(w.reshape(1, feat, m, share), ((0, 0), (0, 0), (0, 0), (0, fill))).reshape(
                1, feat, m * hid_c
            )
            for w in (w_gate, w_up)
        )
        w_down = jnp.pad(
            w_down.reshape(1, m, share, feat), ((0, 0), (0, 0), (0, fill), (0, 0))
        ).reshape(1, m * hid_c, feat)
    wide = -(-slots // LANES) * LANES
    parts = len(spread_tiles(feat // LANES))
    block = LANES * parts
    vmem = pl.BlockSpec(memory_space=pltpu.VMEM)
    hbm = pl.BlockSpec(memory_space=pl.ANY)
    dma = pltpu.SemaphoreType.DMA
    array = jax.ShapeDtypeStruct
    mixed, dots, sel, back = pl.pallas_call(
        functools.partial(layer, n, m),
        out_shape=(
            array((tok, feat), BF16),
            array((top, tok), F32),
            array((slots, tok), BF16),
            array((parts, n, ROWS, LANES), BF16),
        ),
        in_specs=[hbm] * 7,
        out_specs=(hbm, hbm, hbm, hbm),
        scratch_shapes=[
            pltpu.VMEM((tok, feat), BF16),
            pltpu.VMEM((top, tok), jnp.int32),
            pltpu.VMEM((top, tok), F32),
            pltpu.VMEM((tok, feat), BF16),
            pltpu.VMEM((slots, feat), BF16),
            pltpu.VMEM((feat, 2 * m * hid_c), BF16),
            pltpu.VMEM((m * hid_c, feat), BF16),
            pltpu.VMEM((2, n, ROWS, block), BF16),
            pltpu.VMEM((2, n, ROWS, block), BF16),
            pltpu.VMEM((m, slots, 2 * hid_c), BF16),
            pltpu.VMEM((m, slots, 2 * hid_c), BF16),
            pltpu.VMEM((m, slots, hid_c), BF16),
            pltpu.VMEM((m, slots, hid_c), BF16),
            pltpu.VMEM((slots, hid_c), BF16),
            pltpu.VMEM((m, slots, hid_c), BF16),
            pltpu.VMEM((slots, 2 * hid_c), BF16),
            pltpu.VMEM((m, slots, 2 * hid_c), BF16),
            pltpu.VMEM((1, wide), F32),
            pltpu.VMEM((m, 1, wide), F32),
            pltpu.VMEM((n, ROWS, block), BF16),
            pltpu.VMEM((parts, n, ROWS, LANES), BF16),
            pltpu.VMEM((n, ROWS, block), BF16),
            pltpu.VMEM((tok, feat), BF16),
            pltpu.VMEM((top, tok), F32),
            pltpu.VMEM((slots, tok), BF16),
            dma((4,)),
            dma((3, m)),
            dma((3 + parts, n)),
            dma((3 + parts, n)),
            dma((5, m)),
            dma((5, m)),
            dma((3 + parts,)),
        ],
        compiler_params=pltpu.CompilerParams(
            collective_id=0, has_side_effects=True, vmem_limit_bytes=56 * 1024 * 1024
        ),
    )(tokens, picks.T, gates.T, w_gate, w_up, w_down, cotangent)
    mixed, grad_tokens, dots = pl.pallas_call(
        finish,
        out_shape=(
            array((tok, feat), BF16),
            array((tok, feat), BF16),
            array((top, tok), F32),
        ),
        in_specs=[vmem] * 4,
        out_specs=(vmem, vmem, vmem),
    )(mixed, dots, sel, back)
    return mixed, grad_tokens, dots.T


def solution(mesh):
    placed = (
        P("dp", "expert"),
        P("dp", None),
        P("dp", None),
        P("dp", "expert", None),
        P("dp", "expert", None),
        P("dp", None, "expert"),
        P("dp", "expert"),
    )
    return jax.shard_map(
        shards,
        mesh=mesh,
        in_specs=placed,
        out_specs=(P("dp", "expert"), P("dp", "expert"), P("dp", None)),
        check_vma=False,
    )
```

```python
import functools

import jax
import jax.numpy as jnp
from jax import lax
from jax.experimental import pallas as pl
from jax.experimental.pallas import tpu as pltpu
from jax.sharding import PartitionSpec as P

CAP = 6
ROWS = 16
LANES = 128
BF16 = jnp.bfloat16
F32 = jnp.float32
NN = (((1,), (0,)), ((), ()))
NT = (((1,), (1,)), ((), ()))
TN = (((0,), (0,)), ((), ()))


def mm(a, b, dims=NN):
    return lax.dot_general(a, b, dims, preferred_element_type=F32)


def iota(shape, dim):
    return lax.broadcasted_iota(jnp.int32, shape, dim)


def onehot(mask):
    return jnp.where(mask, 1.0, 0.0).astype(BF16)


def spread_tiles(tiles):
    wide = -(-tiles * CAP // ROWS)
    return [
        sorted({i // CAP for i in range(w * ROWS, min((w + 1) * ROWS, tiles * CAP))})
        for w in range(wide)
    ]


def sixth(value):
    return (value * 10923) >> 16


def fold_maps(slots, blocks, tiles):
    maps = []
    for w, found in enumerate(spread_tiles(tiles)):
        shape = (blocks * ROWS, len(found) * slots)
        row, lane = iota(shape, 0), iota(shape, 1)
        number = (row & (ROWS - 1)) + w * ROWS
        tile = sixth(number)
        target = (tile - found[0]) * slots + (row >> 4) * CAP + number - tile * CAP
        maps.append(onehot((lane == target) & (number < tiles * CAP)))
    return maps


def fold(maps, value, blocks):
    tiles = value.shape[1] // LANES
    parts = []
    for place, found in zip(maps, spread_tiles(tiles)):
        stack = jnp.concatenate([value[:, t * LANES : (t + 1) * LANES] for t in found], axis=0)
        parts.append(mm(place, stack).astype(BF16))
    return jnp.concatenate(parts, axis=1).reshape(blocks, ROWS, len(parts) * LANES)


def unfold_maps(slots, blocks, tiles):
    shape = (slots, blocks * ROWS)
    slot, lane = iota(shape, 0), iota(shape, 1)
    block = sixth(slot)
    maps = []
    for w, found in enumerate(spread_tiles(tiles)):
        places = []
        for t in found:
            row = slot - block * CAP + (t * CAP - w * ROWS)
            places.append(onehot((lane == block * ROWS + row) & (row >= 0) & (row < ROWS)))
        maps.append(jnp.concatenate(places, axis=0))
    return maps


def unfold(maps, value, slots, tiles):
    value = value.reshape(value.shape[0] * ROWS, value.shape[2])
    out = [None] * tiles
    for w, found in enumerate(spread_tiles(tiles)):
        got = mm(maps[w], value[:, w * LANES : (w + 1) * LANES])
        for p, t in enumerate(found):
            piece = got[p * slots : (p + 1) * slots]
            out[t] = piece if out[t] is None else out[t] + piece
    return jnp.concatenate(out, axis=1).astype(BF16)


def layer(
    n, m, tokens_in, picks_in, gates_in, w_gate, w_up, w_down, cotangent_in,
    mixed_out, dots_done, sel_out, back_grad,
    tokens, picks, gates, cotangent, cot_slot, gu_v, down_v, send, recv, part, part_in, part_h,
    part_h_in, both_v, both_in, grad_v, grad_in, dot_v, dot_in, ret, back, mixed_v, gg_v, sel_v,
    in_sem, w_sem, dp_send, dp_recv, ex_send, ex_recv, out_sem,
):
    me = lax.axis_index("dp")
    mine = lax.axis_index("expert")
    tok, feat = tokens.shape
    tiles = feat // LANES
    top = picks.shape[0]
    slots = n * CAP
    hid_c = grad_v.shape[1]
    wide = dot_v.shape[1]
    near = sorted(range(1, n), key=lambda o: -min(o, n - o))
    steps = [m // 2] + [o for o in range(1, m) if o != m // 2] if m > 1 else []

    def ring(index, step, size):
        return lax.rem(index + (step % size), size)

    def to_dp(phase, o, src, dst, step):
        copy = pltpu.make_async_remote_copy(
            src_ref=src, dst_ref=dst,
            send_sem=dp_send.at[phase, o], recv_sem=dp_recv.at[phase, o],
            device_id={"dp": ring(me, step, n)},
        )
        copy.start()
        return copy

    def to_expert(phase, o, src, dst):
        copy = pltpu.make_async_remote_copy(
            src_ref=src, dst_ref=dst,
            send_sem=ex_send.at[phase, o], recv_sem=ex_recv.at[phase, o],
            device_id={"expert": ring(mine, o, m)},
        )
        copy.start()
        return copy

    def columns(owner, width):
        return pl.ds(pl.multiple_of(owner * width, LANES), width)

    arrive = [
        pltpu.make_async_copy(src, dst, in_sem.at[i])
        for i, (src, dst) in enumerate(
            ((picks_in, picks), (gates_in, gates), (tokens_in, tokens), (cotangent_in, cotangent))
        )
    ]
    for copy in arrive:
        copy.start()
    barrier = pltpu.get_barrier_semaphore()
    for o in range(1, n):
        pl.semaphore_signal(barrier, inc=1, device_id={"dp": ring(me, o, n)})
    for o in range(1, m):
        pl.semaphore_signal(barrier, inc=1, device_id={"expert": ring(mine, o, m)})

    loads = {}
    for o in steps + [0]:
        owner = ring(mine, o, m)
        for i, src in enumerate((w_gate, w_up)):
            at = pl.ds(pl.multiple_of((2 * owner + i) * hid_c, LANES), hid_c)
            loads[i, o] = pltpu.make_async_copy(
                src.at[0, :, columns(owner, hid_c)], gu_v.at[:, at], w_sem.at[i, o]
            )
            loads[i, o].start()
    for o in steps + [0]:
        rows = columns(ring(mine, o, m), hid_c)
        loads[2, o] = pltpu.make_async_copy(w_down.at[0, rows, :], down_v.at[rows, :], w_sem.at[2, o])
        loads[2, o].start()
    for copy in arrive[:2]:
        copy.wait()

    slot = iota((slots, tok), 0)
    offset = sixth(slot)
    place = slot - offset * CAP
    named = me + offset
    named = jnp.where(named >= n, named - n, named)
    picked = jnp.zeros((slots, tok), F32)
    gate_of = jnp.zeros((slots, tok), F32)
    for k in range(top):
        hit = picks[k : k + 1, :] == named
        picked = jnp.where(hit, 1.0, picked)
        gate_of = jnp.where(hit, gates[k : k + 1, :], gate_of)
    earlier = onehot(iota((tok, tok), 0) < iota((tok, tok), 1))
    rank = mm(picked.astype(BF16), earlier)
    chosen = (picked > 0.5) & (rank == place.astype(F32))
    sel = onehot(chosen)
    weight = jnp.where(chosen, gate_of, 0.0)
    folds = fold_maps(slots, n, tiles)
    arrive[2].wait()
    send[0] = fold(folds, mm(sel, tokens[...]).astype(BF16), n)

    pl.semaphore_wait(barrier, n - 1 + m - 1)
    tok_out = [to_dp(0, o, send.at[0, o], recv.at[0, o], o) for o in near]
    slot_gate = jnp.sum(weight, axis=1, keepdims=True)
    arrive[3].wait()
    chosen_cot = mm(sel, cotangent[...])
    send[1] = fold(folds, (chosen_cot * slot_gate).astype(BF16), n)
    cot_out = [to_dp(1, o, send.at[1, o], recv.at[1, o], o) for o in near]
    recv[0, 0] = send[0, 0]
    recv[1, 0] = send[1, 0]
    cot_slot[...] = chosen_cot.astype(BF16)

    sel_v[...] = sel
    save_sel = pltpu.make_async_copy(sel_v, sel_out, out_sem.at[0])
    save_sel.start()
    unfolds = unfold_maps(slots, n, tiles)

    for copy in tok_out:
        copy.wait_recv()
    x_tok = unfold(unfolds, recv[0], slots, tiles)
    summing = []
    for o in steps:
        loads[0, o].wait()
        loads[1, o].wait()
        part[o] = mm(x_tok, gu_v[:, columns(ring(mine, o, m), 2 * hid_c)]).astype(BF16)
        summing.append(to_expert(0, o, part.at[o], part_in.at[o]))
    loads[0, 0].wait()
    loads[1, 0].wait()
    both = mm(x_tok, gu_v[:, columns(mine, 2 * hid_c)])

    for copy in cot_out:
        copy.wait_recv()
    x_cot = unfold(unfolds, recv[1], slots, tiles)
    summing_h = []
    for o in steps:
        loads[2, o].wait()
        part_h[o] = mm(x_cot, down_v[columns(ring(mine, o, m), hid_c), :], NT).astype(BF16)
        summing_h.append(to_expert(1, o, part_h.at[o], part_h_in.at[o]))
    loads[2, 0].wait()
    grad_hidden = mm(x_cot, down_v[columns(mine, hid_c), :], NT)

    def activation(both):
        gate_pre, up_pre = both[:, :hid_c], both[:, hid_c:]
        logistic = jax.nn.sigmoid(gate_pre)
        silu = gate_pre * logistic
        slope = up_pre * (logistic * (1.0 + gate_pre * (1.0 - logistic)))
        return (silu * up_pre).astype(BF16), silu, slope

    def backward(grad_hidden, silu, slope, owner):
        pair = jnp.concatenate([grad_hidden * slope, grad_hidden * silu], axis=1).astype(BF16)
        return mm(pair, gu_v[:, columns(owner, 2 * hid_c)], NT)

    for o, copy in zip(steps, summing):
        copy.wait_recv()
        both += part_in[o].astype(F32)
    both_v[...] = both.astype(BF16)
    spread = [to_expert(2, o, both_v, both_in.at[o]) for o in steps]
    act, silu, slope = activation(both)
    out = mm(act, down_v[columns(mine, hid_c), :])
    for o, copy in zip(steps, summing_h):
        copy.wait_recv()
        grad_hidden += part_h_in[o].astype(F32)
    grad_v[...] = grad_hidden.astype(BF16)
    spread_grad = [to_expert(3, o, grad_v, grad_in.at[o]) for o in steps]
    grad = backward(grad_hidden, silu, slope, mine)
    saved = {}
    for o, copy in reversed(list(zip(steps, spread))):
        copy.wait_recv()
        act, *saved[o] = activation(both_in[o].astype(F32))
        out += mm(act, down_v[columns(ring(mine, m - o, m), hid_c), :])
    ret[0] = fold(folds, out.astype(BF16), n)
    out_home = [to_dp(2, o, ret.at[0, o], back.at[o], n - o) for o in near]
    back[0] = ret[0, 0]
    for o, copy in reversed(list(zip(steps, spread_grad))):
        copy.wait_recv()
        grad += backward(grad_in[o].astype(F32), *saved[o], ring(mine, m - o, m))
    ret[1] = fold(folds, grad.astype(BF16), n)
    grad_home = [to_dp(3, o, ret.at[1, o], back_grad.at[o], n - o) for o in near]
    keep = pltpu.make_async_copy(ret.at[1, 0], back_grad.at[0], out_sem.at[1])
    keep.start()

    for copy in out_home:
        copy.wait_recv()
    y_out = unfold(unfolds, back[...], slots, tiles)
    dots = cot_slot[...].astype(F32) * y_out.astype(F32)
    dots = jnp.sum(dots, axis=1, keepdims=True)
    diag = iota((slots, wide), 0) == iota((slots, wide), 1)
    dots = jnp.sum(jnp.where(diag, dots, 0.0), axis=0, keepdims=True)
    dot_v[...] = dots
    spread_dot = [to_expert(4, o, dot_v, dot_in.at[o]) for o in steps]
    weight_hi = weight.astype(BF16)
    weight_lo = (weight - weight_hi.astype(F32)).astype(BF16)
    mixed_v[...] = (mm(weight_hi, y_out, TN) + mm(weight_lo, y_out, TN)).astype(BF16)
    save_mixed = pltpu.make_async_copy(mixed_v, mixed_out, out_sem.at[2])
    save_mixed.start()
    for copy in tok_out + cot_out + summing + summing_h + spread + spread_grad + out_home:
        copy.wait_send()
    for o, copy in zip(steps, spread_dot):
        copy.wait_recv()
        dots += dot_in[o]
    dots = jnp.sum(jnp.where(diag, dots, 0.0), axis=1, keepdims=True)
    value = jnp.where(chosen, dots, 0.0)
    for k in range(top):
        hit = picks[k : k + 1, :] == named
        gg_v[k : k + 1, :] = jnp.sum(jnp.where(hit, value, 0.0), axis=0, keepdims=True)
    save_gg = pltpu.make_async_copy(gg_v, dots_done, out_sem.at[3])
    save_gg.start()

    for copy in (save_sel, keep, save_mixed):
        copy.wait()
    for copy in spread_dot + grad_home:
        copy.wait_send()
    for copy in grad_home:
        copy.wait_recv()
    save_gg.wait()


def finish(mixed, dots, sel, back, mixed_out, grad_tokens, grad_gates):
    blocks = back.shape[0]
    slots = sel.shape[0]
    tiles = mixed.shape[1] // LANES
    y_grad = unfold(unfold_maps(slots, blocks, tiles), back[...], slots, tiles)
    grad_tokens[...] = mm(sel[...], y_grad, TN).astype(BF16)
    mixed_out[...] = mixed[...]
    grad_gates[...] = dots[...]


def shards(tokens, picks, gates, w_gate, w_up, w_down, cotangent):
    n = lax.axis_size("dp")
    m = lax.axis_size("expert")
    tok, feat = tokens.shape
    top = picks.shape[1]
    hidden = w_gate.shape[2]
    slots = n * CAP
    share = hidden // m
    hid_c = -(-share // LANES) * LANES
    if hid_c != share:
        fill = hid_c - share
        w_gate, w_up = (
            jnp.pad(w.reshape(1, feat, m, share), ((0, 0), (0, 0), (0, 0), (0, fill))).reshape(
                1, feat, m * hid_c
            )
            for w in (w_gate, w_up)
        )
        w_down = jnp.pad(
            w_down.reshape(1, m, share, feat), ((0, 0), (0, 0), (0, fill), (0, 0))
        ).reshape(1, m * hid_c, feat)
    wide = -(-slots // LANES) * LANES
    block = LANES * len(spread_tiles(feat // LANES))
    vmem = pl.BlockSpec(memory_space=pltpu.VMEM)
    hbm = pl.BlockSpec(memory_space=pl.ANY)
    dma = pltpu.SemaphoreType.DMA
    array = jax.ShapeDtypeStruct
    mixed, dots, sel, back = pl.pallas_call(
        functools.partial(layer, n, m),
        out_shape=(
            array((tok, feat), BF16),
            array((top, tok), F32),
            array((slots, tok), BF16),
            array((n, ROWS, block), BF16),
        ),
        in_specs=[hbm] * 7,
        out_specs=(hbm, hbm, hbm, hbm),
        scratch_shapes=[
            pltpu.VMEM((tok, feat), BF16),
            pltpu.VMEM((top, tok), jnp.int32),
            pltpu.VMEM((top, tok), F32),
            pltpu.VMEM((tok, feat), BF16),
            pltpu.VMEM((slots, feat), BF16),
            pltpu.VMEM((feat, 2 * m * hid_c), BF16),
            pltpu.VMEM((m * hid_c, feat), BF16),
            pltpu.VMEM((2, n, ROWS, block), BF16),
            pltpu.VMEM((2, n, ROWS, block), BF16),
            pltpu.VMEM((m, slots, 2 * hid_c), BF16),
            pltpu.VMEM((m, slots, 2 * hid_c), BF16),
            pltpu.VMEM((m, slots, hid_c), BF16),
            pltpu.VMEM((m, slots, hid_c), BF16),
            pltpu.VMEM((slots, 2 * hid_c), BF16),
            pltpu.VMEM((m, slots, 2 * hid_c), BF16),
            pltpu.VMEM((slots, hid_c), BF16),
            pltpu.VMEM((m, slots, hid_c), BF16),
            pltpu.VMEM((1, wide), F32),
            pltpu.VMEM((m, 1, wide), F32),
            pltpu.VMEM((2, n, ROWS, block), BF16),
            pltpu.VMEM((n, ROWS, block), BF16),
            pltpu.VMEM((tok, feat), BF16),
            pltpu.VMEM((top, tok), F32),
            pltpu.VMEM((slots, tok), BF16),
            dma((4,)),
            dma((3, m)),
            dma((4, n)),
            dma((4, n)),
            dma((5, m)),
            dma((5, m)),
            dma((4,)),
        ],
        compiler_params=pltpu.CompilerParams(
            collective_id=0, has_side_effects=True, vmem_limit_bytes=56 * 1024 * 1024
        ),
    )(tokens, picks.T, gates.T, w_gate, w_up, w_down, cotangent)
    mixed, grad_tokens, dots = pl.pallas_call(
        finish,
        out_shape=(
            array((tok, feat), BF16),
            array((tok, feat), BF16),
            array((top, tok), F32),
        ),
        in_specs=[vmem] * 4,
        out_specs=(vmem, vmem, vmem),
    )(mixed, dots, sel, back)
    return mixed, grad_tokens, dots.T


def solution(mesh):
    placed = (
        P("dp", "expert"),
        P("dp", None),
        P("dp", None),
        P("dp", "expert", None),
        P("dp", "expert", None),
        P("dp", None, "expert"),
        P("dp", "expert"),
    )
    return jax.shard_map(
        shards,
        mesh=mesh,
        in_specs=placed,
        out_specs=(P("dp", "expert"), P("dp", "expert"), P("dp", None)),
        check_vma=False,
    )
```

```python
import functools

import jax
import jax.numpy as jnp
from jax import lax
from jax.experimental import pallas as pl
from jax.experimental.pallas import tpu as pltpu
from jax.sharding import PartitionSpec as P

CAP = 6
ROWS = 16
LANES = 128
BF16 = jnp.bfloat16
F32 = jnp.float32
NN = (((1,), (0,)), ((), ()))
NT = (((1,), (1,)), ((), ()))
TN = (((0,), (0,)), ((), ()))


def mm(a, b, dims=NN):
    return lax.dot_general(a, b, dims, preferred_element_type=F32)


def iota(shape, dim):
    return lax.broadcasted_iota(jnp.int32, shape, dim)


def onehot(mask):
    return jnp.where(mask, 1.0, 0.0).astype(BF16)


def spread_tiles(tiles):
    wide = -(-tiles * CAP // ROWS)
    return [
        sorted({i // CAP for i in range(w * ROWS, min((w + 1) * ROWS, tiles * CAP))})
        for w in range(wide)
    ]


def sixth(value):
    return (value * 10923) >> 16


def fold_maps(slots, blocks, tiles):
    maps = []
    for w, found in enumerate(spread_tiles(tiles)):
        shape = (blocks * ROWS, len(found) * slots)
        row, lane = iota(shape, 0), iota(shape, 1)
        number = (row & (ROWS - 1)) + w * ROWS
        tile = sixth(number)
        target = (tile - found[0]) * slots + (row >> 4) * CAP + number - tile * CAP
        maps.append(onehot((lane == target) & (number < tiles * CAP)))
    return maps


def cut(value):
    return [value[:, at : at + LANES] for at in range(0, value.shape[1], LANES)]


def fold_one(place, tiles, blocks):
    return mm(place, jnp.concatenate(tiles, axis=0)).astype(BF16).reshape(blocks, ROWS, LANES)


def fold(maps, value, blocks):
    value = cut(value)
    parts = [
        fold_one(place, [value[t] for t in found], blocks)
        for place, found in zip(maps, spread_tiles(len(value)))
    ]
    return jnp.concatenate(parts, axis=2)


def unfold_maps(slots, blocks, tiles):
    shape = (slots, blocks * ROWS)
    slot, lane = iota(shape, 0), iota(shape, 1)
    block = sixth(slot)
    maps = []
    for w, found in enumerate(spread_tiles(tiles)):
        places = []
        for t in found:
            row = slot - block * CAP + (t * CAP - w * ROWS)
            places.append(onehot((lane == block * ROWS + row) & (row >= 0) & (row < ROWS)))
        maps.append(jnp.concatenate(places, axis=0))
    return maps


def unfold(maps, value, slots, tiles):
    out = [None] * tiles
    for w, found in enumerate(spread_tiles(tiles)):
        part = value[:, :, w * LANES : (w + 1) * LANES] if len(value.shape) == 3 else value[w]
        got = mm(maps[w], part.reshape(part.shape[0] * ROWS, LANES))
        for p, t in enumerate(found):
            piece = got[p * slots : (p + 1) * slots]
            out[t] = piece if out[t] is None else out[t] + piece
    return jnp.concatenate(out, axis=1).astype(BF16)


def layer(
    n, m, tokens_in, picks_in, gates_in, w_gate, w_up, w_down, cotangent_in,
    mixed_out, dots_out, slot_out, sel_out, back_grad,
    tokens, picks, gates, cotangent, cot_slot, gu_v, down_v, send, recv, part, part_in, part_h,
    part_h_in, act_v, act_in, grad_v, grad_in, dot_v, ret, ret_grad, back, mixed_v, slot_v,
    sel_v,
    in_sem, w_sem, dp_send, dp_recv, ex_send, ex_recv, out_sem,
):
    me = lax.axis_index("dp")
    mine = lax.axis_index("expert")
    tok, feat = tokens.shape
    tiles = feat // LANES
    top = picks.shape[0]
    slots = n * CAP
    hid_c = act_v.shape[1]
    wide = dot_v.shape[1]
    near = sorted(range(1, n), key=lambda o: -min(o, n - o))
    steps = [m // 2] + [o for o in range(1, m) if o != m // 2] if m > 1 else []

    def ring(index, step, size):
        return lax.rem(index + (step % size), size)

    def to_dp(phase, o, src, dst, step):
        copy = pltpu.make_async_remote_copy(
            src_ref=src, dst_ref=dst,
            send_sem=dp_send.at[phase, o], recv_sem=dp_recv.at[phase, o],
            device_id={"dp": ring(me, step, n)},
        )
        copy.start()
        return copy

    def to_expert(phase, o, src, dst):
        copy = pltpu.make_async_remote_copy(
            src_ref=src, dst_ref=dst,
            send_sem=ex_send.at[phase, o], recv_sem=ex_recv.at[phase, o],
            device_id={"expert": ring(mine, o, m)},
        )
        copy.start()
        return copy

    def columns(owner, width):
        return pl.ds(pl.multiple_of(owner * width, LANES), width)

    arrive = [
        pltpu.make_async_copy(src, dst, in_sem.at[i])
        for i, (src, dst) in enumerate(
            ((picks_in, picks), (gates_in, gates), (tokens_in, tokens), (cotangent_in, cotangent))
        )
    ]
    for copy in arrive:
        copy.start()
    barrier = pltpu.get_barrier_semaphore()
    for o in range(1, n):
        pl.semaphore_signal(barrier, inc=1, device_id={"dp": ring(me, o, n)})
    for o in range(1, m):
        pl.semaphore_signal(barrier, inc=1, device_id={"expert": ring(mine, o, m)})

    loads = {}
    for o in steps + [0]:
        owner = ring(mine, o, m)
        for i, src in enumerate((w_gate, w_up)):
            at = pl.ds(pl.multiple_of((2 * owner + i) * hid_c, LANES), hid_c)
            loads[i, o] = pltpu.make_async_copy(
                src.at[0, :, columns(owner, hid_c)], gu_v.at[:, at], w_sem.at[i, o]
            )
            loads[i, o].start()
    for o in steps + [0]:
        rows = columns(ring(mine, o, m), hid_c)
        loads[2, o] = pltpu.make_async_copy(w_down.at[0, rows, :], down_v.at[rows, :], w_sem.at[2, o])
        loads[2, o].start()
    for copy in arrive[:2]:
        copy.wait()

    slot = iota((slots, tok), 0)
    offset = sixth(slot)
    place = slot - offset * CAP
    named = me + offset
    named = jnp.where(named >= n, named - n, named)
    picked = jnp.zeros((slots, tok), F32)
    gate_of = jnp.zeros((slots, tok), F32)
    for k in range(top):
        hit = picks[k : k + 1, :] == named
        picked = jnp.where(hit, 1.0, picked)
        gate_of = jnp.where(hit, gates[k : k + 1, :], gate_of)
    earlier = onehot(iota((tok, tok), 0) < iota((tok, tok), 1))
    rank = mm(picked.astype(BF16), earlier)
    chosen = (picked > 0.5) & (rank == place.astype(F32))
    sel = onehot(chosen)
    weight = jnp.where(chosen, gate_of, 0.0)
    folds = fold_maps(slots, n, tiles)
    arrive[2].wait()
    send[0] = fold(folds, mm(sel, tokens[...]).astype(BF16), n)

    pl.semaphore_wait(barrier, n - 1 + m - 1)
    tok_out = [to_dp(0, o, send.at[0, o], recv.at[0, o], o) for o in near]
    slot_gate = jnp.sum(weight, axis=1, keepdims=True)
    arrive[3].wait()
    chosen_cot = mm(sel, cotangent[...])
    send[1] = fold(folds, (chosen_cot * slot_gate).astype(BF16), n)
    cot_out = [to_dp(1, o, send.at[1, o], recv.at[1, o], o) for o in near]
    recv[0, 0] = send[0, 0]
    recv[1, 0] = send[1, 0]
    cot_slot[...] = chosen_cot.astype(BF16)

    sel_v[...] = sel
    save_sel = pltpu.make_async_copy(sel_v, sel_out, out_sem.at[0])
    save_sel.start()
    unfolds = unfold_maps(slots, n, tiles)
    for k in range(top):
        hit = chosen & (picks[k : k + 1, :] == named)
        number = jnp.where(hit, slot.astype(F32) + 1.0, 0.0)
        slot_v[k : k + 1, :] = jnp.sum(number, axis=0, keepdims=True) - 1.0
    save_slot = pltpu.make_async_copy(slot_v, slot_out, out_sem.at[3 + len(folds)])
    save_slot.start()

    for copy in tok_out:
        copy.wait_recv()
    x_tok = unfold(unfolds, recv[0], slots, tiles)
    summing = []
    for o in steps:
        loads[0, o].wait()
        loads[1, o].wait()
        part[o] = mm(x_tok, gu_v[:, columns(ring(mine, o, m), 2 * hid_c)]).astype(BF16)
        summing.append(to_expert(0, o, part.at[o], part_in.at[o]))
    loads[0, 0].wait()
    loads[1, 0].wait()
    both = mm(x_tok, gu_v[:, columns(mine, 2 * hid_c)])

    for copy in cot_out:
        copy.wait_recv()
    x_cot = unfold(unfolds, recv[1], slots, tiles)
    summing_h = []
    for o in steps:
        loads[2, o].wait()
        part_h[o] = mm(x_cot, down_v[columns(ring(mine, o, m), hid_c), :], NT).astype(BF16)
        summing_h.append(to_expert(1, o, part_h.at[o], part_h_in.at[o]))
    loads[2, 0].wait()
    grad_hidden = mm(x_cot, down_v[columns(mine, hid_c), :], NT)

    for o, copy in zip(steps, summing):
        copy.wait_recv()
        both += part_in[o].astype(F32)
    gate_pre = both[:, :hid_c]
    up_pre = both[:, hid_c:]
    logistic = jax.nn.sigmoid(gate_pre)
    silu = gate_pre * logistic
    act = (silu * up_pre).astype(BF16)
    act_v[...] = act
    spread_act = [to_expert(2, o, act_v, act_in.at[o]) for o in steps]
    slope = up_pre * (logistic * (1.0 + gate_pre * (1.0 - logistic)))
    for o, copy in zip(steps, summing_h):
        copy.wait_recv()
        grad_hidden += part_h_in[o].astype(F32)
    grad_v[:, :hid_c] = (grad_hidden * slope).astype(BF16)
    grad_v[:, hid_c:] = (grad_hidden * silu).astype(BF16)
    spread_grad = [to_expert(3, o, grad_v, grad_in.at[o]) for o in steps]
    out = mm(act, down_v[columns(mine, hid_c), :])
    for o, copy in reversed(list(zip(steps, spread_act))):
        copy.wait_recv()
        out += mm(act_in[o], down_v[columns(ring(mine, m - o, m), hid_c), :])
    ret[...] = fold(folds, out.astype(BF16), n)
    out_home = [to_dp(2, o, ret.at[o], back.at[o], n - o) for o in near]
    back[0] = ret[0]
    own_grad = mm(grad_v[...], gu_v[:, columns(mine, 2 * hid_c)], NT)
    for copy in spread_grad:
        copy.wait_recv()
    grad = []
    grad_home = []
    keep = []
    for w, found in enumerate(spread_tiles(tiles)):
        rows = slice(len(grad) * LANES, (found[-1] + 1) * LANES)
        piece = own_grad[:, rows]
        for o in steps:
            at = columns(ring(mine, m - o, m), 2 * hid_c)
            piece += mm(grad_in[o], gu_v[rows, at], NT)
        grad += cut(piece.astype(BF16))
        ret_grad[w] = fold_one(folds[w], [grad[t] for t in found], n)
        for o in near:
            grad_home.append(to_dp(3 + w, o, ret_grad.at[w, o], back_grad.at[w, o], n - o))
        keep.append(pltpu.make_async_copy(ret_grad.at[w, 0], back_grad.at[w, 0], out_sem.at[2 + w]))
        keep[w].start()

    for copy in out_home:
        copy.wait_recv()
    y_out = unfold(unfolds, back[...], slots, tiles)
    dots = cot_slot[...].astype(F32) * y_out.astype(F32)
    dots = jnp.sum(dots, axis=1, keepdims=True)
    diag = iota((slots, wide), 0) == iota((slots, wide), 1)
    dots = jnp.sum(jnp.where(diag, dots, 0.0), axis=0, keepdims=True)
    dot_v[...] = dots
    spread_dot = [to_expert(4, o, dot_v, dots_out.at[o]) for o in steps]
    save_dot = pltpu.make_async_copy(dot_v, dots_out.at[0], out_sem.at[2 + len(keep)])
    save_dot.start()
    weight_hi = weight.astype(BF16)
    weight_lo = (weight - weight_hi.astype(F32)).astype(BF16)
    mixed_v[...] = (mm(weight_hi, y_out, TN) + mm(weight_lo, y_out, TN)).astype(BF16)
    save_mixed = pltpu.make_async_copy(mixed_v, mixed_out, out_sem.at[1])
    save_mixed.start()
    for copy in tok_out + cot_out + summing + summing_h + spread_act + spread_grad + out_home:
        copy.wait_send()
    for copy in [save_sel, save_slot, save_mixed, save_dot] + keep:
        copy.wait()
    for copy in spread_dot + grad_home:
        copy.wait_send()
    for copy in spread_dot + grad_home:
        copy.wait_recv()


def finish(mixed, dots, slot, sel, back, mixed_out, grad_tokens, grad_gates):
    blocks = back.shape[1]
    slots, tok = sel.shape
    tiles = mixed.shape[1] // LANES
    y_grad = unfold(unfold_maps(slots, blocks, tiles), back[...], slots, tiles)
    grad_tokens[...] = mm(sel[...], y_grad, TN).astype(BF16)
    mixed_out[...] = mixed[...]
    total = dots[0]
    for o in range(1, dots.shape[0]):
        total += dots[o]
    diag = iota((slots, total.shape[1]), 0) == iota((slots, total.shape[1]), 1)
    total = jnp.sum(jnp.where(diag, total, 0.0), axis=1, keepdims=True)
    number = iota((slots, tok), 0).astype(F32)
    for k in range(slot.shape[0]):
        value = jnp.where(slot[k : k + 1, :] == number, total, 0.0)
        grad_gates[k : k + 1, :] = jnp.sum(value, axis=0, keepdims=True)


def shards(tokens, picks, gates, w_gate, w_up, w_down, cotangent):
    n = lax.axis_size("dp")
    m = lax.axis_size("expert")
    tok, feat = tokens.shape
    top = picks.shape[1]
    hidden = w_gate.shape[2]
    slots = n * CAP
    share = hidden // m
    hid_c = -(-share // LANES) * LANES
    if hid_c != share:
        fill = hid_c - share
        w_gate, w_up = (
            jnp.pad(w.reshape(1, feat, m, share), ((0, 0), (0, 0), (0, 0), (0, fill))).reshape(
                1, feat, m * hid_c
            )
            for w in (w_gate, w_up)
        )
        w_down = jnp.pad(
            w_down.reshape(1, m, share, feat), ((0, 0), (0, 0), (0, fill), (0, 0))
        ).reshape(1, m * hid_c, feat)
    wide = -(-slots // LANES) * LANES
    parts = len(spread_tiles(feat // LANES))
    block = LANES * parts
    vmem = pl.BlockSpec(memory_space=pltpu.VMEM)
    hbm = pl.BlockSpec(memory_space=pl.ANY)
    dma = pltpu.SemaphoreType.DMA
    array = jax.ShapeDtypeStruct
    mixed, dots, slot, sel, back = pl.pallas_call(
        functools.partial(layer, n, m),
        out_shape=(
            array((tok, feat), BF16),
            array((m, 1, wide), F32),
            array((top, tok), F32),
            array((slots, tok), BF16),
            array((parts, n, ROWS, LANES), BF16),
        ),
        in_specs=[hbm] * 7,
        out_specs=(hbm,) * 5,
        scratch_shapes=[
            pltpu.VMEM((tok, feat), BF16),
            pltpu.VMEM((top, tok), jnp.int32),
            pltpu.VMEM((top, tok), F32),
            pltpu.VMEM((tok, feat), BF16),
            pltpu.VMEM((slots, feat), BF16),
            pltpu.VMEM((feat, 2 * m * hid_c), BF16),
            pltpu.VMEM((m * hid_c, feat), BF16),
            pltpu.VMEM((2, n, ROWS, block), BF16),
            pltpu.VMEM((2, n, ROWS, block), BF16),
            pltpu.VMEM((m, slots, 2 * hid_c), BF16),
            pltpu.VMEM((m, slots, 2 * hid_c), BF16),
            pltpu.VMEM((m, slots, hid_c), BF16),
            pltpu.VMEM((m, slots, hid_c), BF16),
            pltpu.VMEM((slots, hid_c), BF16),
            pltpu.VMEM((m, slots, hid_c), BF16),
            pltpu.VMEM((slots, 2 * hid_c), BF16),
            pltpu.VMEM((m, slots, 2 * hid_c), BF16),
            pltpu.VMEM((1, wide), F32),
            pltpu.VMEM((n, ROWS, block), BF16),
            pltpu.VMEM((parts, n, ROWS, LANES), BF16),
            pltpu.VMEM((n, ROWS, block), BF16),
            pltpu.VMEM((tok, feat), BF16),
            pltpu.VMEM((top, tok), F32),
            pltpu.VMEM((slots, tok), BF16),
            dma((4,)),
            dma((3, m)),
            dma((3 + parts, n)),
            dma((3 + parts, n)),
            dma((5, m)),
            dma((5, m)),
            dma((4 + parts,)),
        ],
        compiler_params=pltpu.CompilerParams(
            collective_id=0, has_side_effects=True, vmem_limit_bytes=56 * 1024 * 1024
        ),
    )(tokens, picks.T, gates.T, w_gate, w_up, w_down, cotangent)
    mixed, grad_tokens, dots = pl.pallas_call(
        finish,
        out_shape=(
            array((tok, feat), BF16),
            array((tok, feat), BF16),
            array((top, tok), F32),
        ),
        in_specs=[vmem] * 5,
        out_specs=(vmem, vmem, vmem),
    )(mixed, dots, slot, sel, back)
    return mixed, grad_tokens, dots.T


def solution(mesh):
    placed = (
        P("dp", "expert"),
        P("dp", None),
        P("dp", None),
        P("dp", "expert", None),
        P("dp", "expert", None),
        P("dp", None, "expert"),
        P("dp", "expert"),
    )
    return jax.shard_map(
        shards,
        mesh=mesh,
        in_specs=placed,
        out_specs=(P("dp", "expert"), P("dp", "expert"), P("dp", None)),
        check_vma=False,
    )
```

```python
import functools

import jax
import jax.numpy as jnp
from jax import lax
from jax.experimental import pallas as pl
from jax.experimental.pallas import tpu as pltpu
from jax.sharding import PartitionSpec as P

CAP = 6
ROWS = 16
LANES = 128
BF16 = jnp.bfloat16
F32 = jnp.float32
NN = (((1,), (0,)), ((), ()))
NT = (((1,), (1,)), ((), ()))
TN = (((0,), (0,)), ((), ()))


def mm(a, b, dims=NN):
    return lax.dot_general(a, b, dims, preferred_element_type=F32)


def iota(shape, dim):
    return lax.broadcasted_iota(jnp.int32, shape, dim)


def onehot(mask):
    return jnp.where(mask, 1.0, 0.0).astype(BF16)


def spread_tiles(tiles):
    wide = -(-tiles * CAP // ROWS)
    return [
        sorted({i // CAP for i in range(w * ROWS, min((w + 1) * ROWS, tiles * CAP))})
        for w in range(wide)
    ]


def sixth(value):
    return (value * 10923) >> 16


def fold_maps(slots, blocks, tiles):
    maps = []
    for w, found in enumerate(spread_tiles(tiles)):
        shape = (blocks * ROWS, len(found) * slots)
        row, lane = iota(shape, 0), iota(shape, 1)
        number = (row & (ROWS - 1)) + w * ROWS
        tile = sixth(number)
        target = (tile - found[0]) * slots + (row >> 4) * CAP + number - tile * CAP
        maps.append(onehot((lane == target) & (number < tiles * CAP)))
    return maps


def cut(value):
    return [value[:, at : at + LANES] for at in range(0, value.shape[1], LANES)]


def fold_one(place, tiles, blocks):
    return mm(place, jnp.concatenate(tiles, axis=0)).astype(BF16).reshape(blocks, ROWS, LANES)


def fold(maps, value, blocks):
    value = cut(value)
    parts = [
        fold_one(place, [value[t] for t in found], blocks)
        for place, found in zip(maps, spread_tiles(len(value)))
    ]
    return jnp.concatenate(parts, axis=2)


def unfold_maps(slots, blocks, tiles):
    shape = (slots, blocks * ROWS)
    slot, lane = iota(shape, 0), iota(shape, 1)
    block = sixth(slot)
    maps = []
    for w, found in enumerate(spread_tiles(tiles)):
        places = []
        for t in found:
            row = slot - block * CAP + (t * CAP - w * ROWS)
            places.append(onehot((lane == block * ROWS + row) & (row >= 0) & (row < ROWS)))
        maps.append(jnp.concatenate(places, axis=0))
    return maps


def unfold(maps, value, slots, tiles):
    out = [None] * tiles
    for w, found in enumerate(spread_tiles(tiles)):
        part = value[:, :, w * LANES : (w + 1) * LANES] if len(value.shape) == 3 else value[w]
        got = mm(maps[w], part.reshape(part.shape[0] * ROWS, LANES))
        for p, t in enumerate(found):
            piece = got[p * slots : (p + 1) * slots]
            out[t] = piece if out[t] is None else out[t] + piece
    return jnp.concatenate(out, axis=1).astype(BF16)


def layer(
    n, m, tokens_in, picks_in, gates_in, w_gate, w_up, w_down, cotangent_in,
    mixed_out, dots_out, slot_out, sel_out, back_grad,
    tokens, picks, gates, cotangent, cot_slot, gu_v, down_v, send, recv, part, part_in, part_h,
    part_h_in, act_v, act_in, grad_v, grad_in, dot_v, ret, ret_grad, back, mixed_v, slot_v,
    sel_v,
    in_sem, w_sem, dp_send, dp_recv, ex_send, ex_recv, out_sem,
):
    me = lax.axis_index("dp")
    mine = lax.axis_index("expert")
    tok, feat = tokens.shape
    tiles = feat // LANES
    top = picks.shape[0]
    slots = n * CAP
    hid_c = act_v.shape[1]
    wide = dot_v.shape[1]
    near = sorted(range(1, n), key=lambda o: -min(o, n - o))
    steps = [m // 2] + [o for o in range(1, m) if o != m // 2] if m > 1 else []

    def ring(index, step, size):
        return lax.rem(index + (step % size), size)

    def to_dp(phase, o, src, dst, step):
        copy = pltpu.make_async_remote_copy(
            src_ref=src, dst_ref=dst,
            send_sem=dp_send.at[phase, o], recv_sem=dp_recv.at[phase, o],
            device_id={"dp": ring(me, step, n)},
        )
        copy.start()
        return copy

    def to_expert(phase, o, src, dst):
        copy = pltpu.make_async_remote_copy(
            src_ref=src, dst_ref=dst,
            send_sem=ex_send.at[phase, o], recv_sem=ex_recv.at[phase, o],
            device_id={"expert": ring(mine, o, m)},
        )
        copy.start()
        return copy

    def columns(owner, width):
        return pl.ds(pl.multiple_of(owner * width, LANES), width)

    arrive = [
        pltpu.make_async_copy(src, dst, in_sem.at[i])
        for i, (src, dst) in enumerate(
            ((picks_in, picks), (gates_in, gates), (tokens_in, tokens), (cotangent_in, cotangent))
        )
    ]
    for copy in arrive:
        copy.start()
    barrier = pltpu.get_barrier_semaphore()
    for o in range(1, n):
        pl.semaphore_signal(barrier, inc=1, device_id={"dp": ring(me, o, n)})
    for o in range(1, m):
        pl.semaphore_signal(barrier, inc=1, device_id={"expert": ring(mine, o, m)})

    loads = {}
    for o in steps + [0]:
        owner = ring(mine, o, m)
        for i, src in enumerate((w_gate, w_up)):
            at = pl.ds(pl.multiple_of((2 * owner + i) * hid_c, LANES), hid_c)
            loads[i, o] = pltpu.make_async_copy(
                src.at[0, :, columns(owner, hid_c)], gu_v.at[:, at], w_sem.at[i, o]
            )
            loads[i, o].start()
    for o in steps + [0]:
        rows = columns(ring(mine, o, m), hid_c)
        loads[2, o] = pltpu.make_async_copy(w_down.at[0, rows, :], down_v.at[rows, :], w_sem.at[2, o])
        loads[2, o].start()
    for copy in arrive[:2]:
        copy.wait()

    slot = iota((slots, tok), 0)
    offset = sixth(slot)
    place = slot - offset * CAP
    named = me + offset
    named = jnp.where(named >= n, named - n, named)
    picked = jnp.zeros((slots, tok), F32)
    gate_of = jnp.zeros((slots, tok), F32)
    for k in range(top):
        hit = picks[k : k + 1, :] == named
        picked = jnp.where(hit, 1.0, picked)
        gate_of = jnp.where(hit, gates[k : k + 1, :], gate_of)
    earlier = onehot(iota((tok, tok), 0) < iota((tok, tok), 1))
    rank = mm(picked.astype(BF16), earlier)
    chosen = (picked > 0.5) & (rank == place.astype(F32))
    sel = onehot(chosen)
    weight = jnp.where(chosen, gate_of, 0.0)
    folds = fold_maps(slots, n, tiles)
    arrive[2].wait()
    send[0] = fold(folds, mm(sel, tokens[...]).astype(BF16), n)

    pl.semaphore_wait(barrier, n - 1 + m - 1)
    tok_out = [to_dp(0, o, send.at[0, o], recv.at[0, o], o) for o in near]
    slot_gate = jnp.sum(weight, axis=1, keepdims=True)
    arrive[3].wait()
    chosen_cot = mm(sel, cotangent[...])
    send[1] = fold(folds, (chosen_cot * slot_gate).astype(BF16), n)
    cot_out = [to_dp(1, o, send.at[1, o], recv.at[1, o], o) for o in near]
    recv[0, 0] = send[0, 0]
    recv[1, 0] = send[1, 0]
    cot_slot[...] = chosen_cot.astype(BF16)

    sel_v[...] = sel
    save_sel = pltpu.make_async_copy(sel_v, sel_out, out_sem.at[0])
    save_sel.start()
    unfolds = unfold_maps(slots, n, tiles)
    for k in range(top):
        hit = chosen & (picks[k : k + 1, :] == named)
        number = jnp.where(hit, slot.astype(F32) + 1.0, 0.0)
        slot_v[k : k + 1, :] = jnp.sum(number, axis=0, keepdims=True) - 1.0
    save_slot = pltpu.make_async_copy(slot_v, slot_out, out_sem.at[3 + len(folds)])
    save_slot.start()

    for copy in tok_out:
        copy.wait_recv()
    x_tok = unfold(unfolds, recv[0], slots, tiles)
    summing = []
    for o in steps:
        loads[0, o].wait()
        loads[1, o].wait()
        part[o] = mm(x_tok, gu_v[:, columns(ring(mine, o, m), 2 * hid_c)]).astype(BF16)
        summing.append(to_expert(0, o, part.at[o], part_in.at[o]))
    loads[0, 0].wait()
    loads[1, 0].wait()
    both = mm(x_tok, gu_v[:, columns(mine, 2 * hid_c)])

    for copy in cot_out:
        copy.wait_recv()
    x_cot = unfold(unfolds, recv[1], slots, tiles)
    summing_h = []
    for o in steps:
        loads[2, o].wait()
        part_h[o] = mm(down_v[columns(ring(mine, o, m), hid_c), :], x_cot, NT).T.astype(BF16)
        summing_h.append(to_expert(1, o, part_h.at[o], part_h_in.at[o]))
    loads[2, 0].wait()
    grad_hidden = mm(down_v[columns(mine, hid_c), :], x_cot, NT).T

    for o, copy in zip(steps, summing):
        copy.wait_recv()
        both += part_in[o].astype(F32)
    gate_pre = both[:, :hid_c]
    up_pre = both[:, hid_c:]
    logistic = jax.nn.sigmoid(gate_pre)
    silu = gate_pre * logistic
    act = (silu * up_pre).astype(BF16)
    act_v[...] = act
    spread_act = [to_expert(2, o, act_v, act_in.at[o]) for o in steps]
    slope = up_pre * (logistic * (1.0 + gate_pre * (1.0 - logistic)))
    for o, copy in zip(steps, summing_h):
        copy.wait_recv()
        grad_hidden += part_h_in[o].astype(F32)
    grad_v[:, :hid_c] = (grad_hidden * slope).astype(BF16)
    grad_v[:, hid_c:] = (grad_hidden * silu).astype(BF16)
    spread_grad = [to_expert(3, o, grad_v, grad_in.at[o]) for o in steps]
    out = mm(act, down_v[columns(mine, hid_c), :])
    for o, copy in reversed(list(zip(steps, spread_act))):
        copy.wait_recv()
        out += mm(act_in[o], down_v[columns(ring(mine, m - o, m), hid_c), :])
    ret[...] = fold(folds, out.astype(BF16), n)
    out_home = [to_dp(2, o, ret.at[o], back.at[o], n - o) for o in near]
    back[0] = ret[0]
    own_grad = mm(gu_v[:, columns(mine, 2 * hid_c)], grad_v[...], NT)
    for copy in spread_grad:
        copy.wait_recv()
    grad = []
    grad_home = []
    keep = []
    for w, found in enumerate(spread_tiles(tiles)):
        rows = slice(len(grad) * LANES, (found[-1] + 1) * LANES)
        piece = own_grad[rows]
        for o in steps:
            at = columns(ring(mine, m - o, m), 2 * hid_c)
            piece += mm(gu_v[rows, at], grad_in[o], NT)
        grad += cut(piece.T.astype(BF16))
        ret_grad[w] = fold_one(folds[w], [grad[t] for t in found], n)
        for o in near:
            grad_home.append(to_dp(3 + w, o, ret_grad.at[w, o], back_grad.at[w, o], n - o))
        keep.append(pltpu.make_async_copy(ret_grad.at[w, 0], back_grad.at[w, 0], out_sem.at[2 + w]))
        keep[w].start()

    for copy in out_home:
        copy.wait_recv()
    y_out = unfold(unfolds, back[...], slots, tiles)
    dots = cot_slot[...].astype(F32) * y_out.astype(F32)
    dots = jnp.sum(dots, axis=1, keepdims=True)
    diag = iota((slots, wide), 0) == iota((slots, wide), 1)
    dots = jnp.sum(jnp.where(diag, dots, 0.0), axis=0, keepdims=True)
    dot_v[...] = dots
    spread_dot = [to_expert(4, o, dot_v, dots_out.at[o]) for o in steps]
    save_dot = pltpu.make_async_copy(dot_v, dots_out.at[0], out_sem.at[2 + len(keep)])
    save_dot.start()
    weight_hi = weight.astype(BF16)
    weight_lo = (weight - weight_hi.astype(F32)).astype(BF16)
    mixed_v[...] = (mm(weight_hi, y_out, TN) + mm(weight_lo, y_out, TN)).astype(BF16)
    save_mixed = pltpu.make_async_copy(mixed_v, mixed_out, out_sem.at[1])
    save_mixed.start()
    for copy in tok_out + cot_out + summing + summing_h + spread_act + spread_grad + out_home:
        copy.wait_send()
    for copy in [save_sel, save_slot, save_mixed, save_dot] + keep:
        copy.wait()
    for copy in spread_dot + grad_home:
        copy.wait_send()
    for copy in spread_dot + grad_home:
        copy.wait_recv()


def finish(mixed, dots, slot, sel, back, mixed_out, grad_tokens, grad_gates):
    blocks = back.shape[1]
    slots, tok = sel.shape
    tiles = mixed.shape[1] // LANES
    y_grad = unfold(unfold_maps(slots, blocks, tiles), back[...], slots, tiles)
    grad_tokens[...] = mm(sel[...], y_grad, TN).astype(BF16)
    mixed_out[...] = mixed[...]
    total = dots[0]
    for o in range(1, dots.shape[0]):
        total += dots[o]
    diag = iota((slots, total.shape[1]), 0) == iota((slots, total.shape[1]), 1)
    total = jnp.sum(jnp.where(diag, total, 0.0), axis=1, keepdims=True)
    number = iota((slots, tok), 0).astype(F32)
    for k in range(slot.shape[0]):
        value = jnp.where(slot[k : k + 1, :] == number, total, 0.0)
        grad_gates[k : k + 1, :] = jnp.sum(value, axis=0, keepdims=True)


def shards(tokens, picks, gates, w_gate, w_up, w_down, cotangent):
    n = lax.axis_size("dp")
    m = lax.axis_size("expert")
    tok, feat = tokens.shape
    top = picks.shape[1]
    hidden = w_gate.shape[2]
    slots = n * CAP
    share = hidden // m
    hid_c = -(-share // LANES) * LANES
    if hid_c != share:
        fill = hid_c - share
        w_gate, w_up = (
            jnp.pad(w.reshape(1, feat, m, share), ((0, 0), (0, 0), (0, 0), (0, fill))).reshape(
                1, feat, m * hid_c
            )
            for w in (w_gate, w_up)
        )
        w_down = jnp.pad(
            w_down.reshape(1, m, share, feat), ((0, 0), (0, 0), (0, fill), (0, 0))
        ).reshape(1, m * hid_c, feat)
    wide = -(-slots // LANES) * LANES
    parts = len(spread_tiles(feat // LANES))
    block = LANES * parts
    vmem = pl.BlockSpec(memory_space=pltpu.VMEM)
    hbm = pl.BlockSpec(memory_space=pl.ANY)
    dma = pltpu.SemaphoreType.DMA
    array = jax.ShapeDtypeStruct
    mixed, dots, slot, sel, back = pl.pallas_call(
        functools.partial(layer, n, m),
        out_shape=(
            array((tok, feat), BF16),
            array((m, 1, wide), F32),
            array((top, tok), F32),
            array((slots, tok), BF16),
            array((parts, n, ROWS, LANES), BF16),
        ),
        in_specs=[hbm] * 7,
        out_specs=(hbm,) * 5,
        scratch_shapes=[
            pltpu.VMEM((tok, feat), BF16),
            pltpu.VMEM((top, tok), jnp.int32),
            pltpu.VMEM((top, tok), F32),
            pltpu.VMEM((tok, feat), BF16),
            pltpu.VMEM((slots, feat), BF16),
            pltpu.VMEM((feat, 2 * m * hid_c), BF16),
            pltpu.VMEM((m * hid_c, feat), BF16),
            pltpu.VMEM((2, n, ROWS, block), BF16),
            pltpu.VMEM((2, n, ROWS, block), BF16),
            pltpu.VMEM((m, slots, 2 * hid_c), BF16),
            pltpu.VMEM((m, slots, 2 * hid_c), BF16),
            pltpu.VMEM((m, slots, hid_c), BF16),
            pltpu.VMEM((m, slots, hid_c), BF16),
            pltpu.VMEM((slots, hid_c), BF16),
            pltpu.VMEM((m, slots, hid_c), BF16),
            pltpu.VMEM((slots, 2 * hid_c), BF16),
            pltpu.VMEM((m, slots, 2 * hid_c), BF16),
            pltpu.VMEM((1, wide), F32),
            pltpu.VMEM((n, ROWS, block), BF16),
            pltpu.VMEM((parts, n, ROWS, LANES), BF16),
            pltpu.VMEM((n, ROWS, block), BF16),
            pltpu.VMEM((tok, feat), BF16),
            pltpu.VMEM((top, tok), F32),
            pltpu.VMEM((slots, tok), BF16),
            dma((4,)),
            dma((3, m)),
            dma((3 + parts, n)),
            dma((3 + parts, n)),
            dma((5, m)),
            dma((5, m)),
            dma((4 + parts,)),
        ],
        compiler_params=pltpu.CompilerParams(
            collective_id=0, has_side_effects=True, vmem_limit_bytes=56 * 1024 * 1024
        ),
    )(tokens, picks.T, gates.T, w_gate, w_up, w_down, cotangent)
    mixed, grad_tokens, dots = pl.pallas_call(
        finish,
        out_shape=(
            array((tok, feat), BF16),
            array((tok, feat), BF16),
            array((top, tok), F32),
        ),
        in_specs=[vmem] * 5,
        out_specs=(vmem, vmem, vmem),
    )(mixed, dots, slot, sel, back)
    return mixed, grad_tokens, dots.T


def solution(mesh):
    placed = (
        P("dp", "expert"),
        P("dp", None),
        P("dp", None),
        P("dp", "expert", None),
        P("dp", "expert", None),
        P("dp", None, "expert"),
        P("dp", "expert"),
    )
    return jax.shard_map(
        shards,
        mesh=mesh,
        in_specs=placed,
        out_specs=(P("dp", "expert"), P("dp", "expert"), P("dp", None)),
        check_vma=False,
    )
```
